32 devices in a mesh: trial: 8 (over z, y), geno: 4 (over x, core).
Axes of the slice: x: 2, y: 2, z: 4, core: 2. Of those that a mesh axis runs over, the one named last changes fastest.
Arguments:
- probe_signs: int32 [16, 32, 1, 44, 256], P(None, ('trial', 'geno')), may hold values 0 or 1
- trial_rows: int32 [8], P('trial'), may hold values from 89 to 176
- trial_cols: int32 [8], P('trial'), may hold values from 128 to 256
- ar_rho: float32 [8, 2], P('trial'), may hold values from 0.1 to 0.7
- res_var: float32 [8], P('trial'), may hold values from 4 to 16
- plot_owner: int32 [32, 1, 44, 256, 1], P(('trial', 'geno')), may hold values from 0 to 31; in each aligned block of 11264 rows (0 to 11263, 11264 to 22527, ..., all dimensions but the last counted through in order) at most 704 rows name the same one
- plot_slot: int32 [32, 1, 44, 256], P(('trial', 'geno')), may hold values from 0 to 1023
Outputs:
- geno_terms: float32 [3, 16, 32768], P(None, None, ('trial', 'geno'))
The draws below stay inside these ranges and needn't reach their ends.
Inputs may be any that keep to these rules, and one draw needn't show every extreme that they name: `plot_owner`: among the plot positions of one device at most 704 name the same owner, and in every draw some device has exactly 704 positions for one owner. A plot's genotype is 1024 * plot_owner + plot_slot.
All inputs are finite; a program needn't handle non-finite values. No bound on the sum of `probe_signs` on one device may be relied on, other than what follows from the above.
Results may differ from the reference program's by a relative error of at most 0.0028.
Values may be sent and summed in bfloat16 or wider, within the bound.
No kernel may reach another device: no remote copies, remote signals or barrier semaphores. Data moves between devices by JAX's collectives and lax.ppermute only.
A program may use at most 64 MiB of HBM per device.

```python
import math
import jax
import jax.numpy as jnp
import numpy as np

PROBES = 16
FR = 44
FC = 256
TILES_DEV = 1
G_DEV = 1024
FIELD_ROWS = 176
TRIALS = 8
P_DEV = 11264
CAP = 704
G = 32768
N_TRIAL = 8
N_GENO = 4
DEVICES = 32


def set_ends(entries, rng, smallest, top_value):
    extent = entries.shape
    index_at = [jax.random.randint(jax.random.fold_in(rng, axis), (), 0, extent[axis]) for axis in range(len(extent))]
    entries = entries.at[tuple(index_at)].set(smallest)
    longest = extent.index(max(extent))
    index_at[longest] = (index_at[longest] + 1) % extent[longest]
    return entries.at[tuple(index_at)].set(top_value)


def steps_of(key, extent, cuts, least, largest):
    def one(position, parts):
        draws = jax.random.uniform(jax.random.fold_in(jax.random.fold_in(key, 6), position), (parts,), jnp.float32, least / len(cuts), largest / len(cuts))
        return jnp.repeat(jnp.exp(draws), extent[position] // parts).reshape((-1,) + (1,) * (len(extent) - position - 1))

    loudness = one(*cuts[0])
    for cut in cuts[1:]:
        loudness = loudness * one(*cut)
    return loudness


def shared_out(rng, own, number, rows, count, top, most, skew):
    order = jax.random.permutation(rng, count)
    packed, common = portions_of(count, rows * top, most, skew, True), portions_of(count, rows * top, most, skew, False)
    places = jnp.arange(count)

    def named(sizes, rotation):
        used = int((sizes > 0).sum())
        fixed = max(1, used // 4)
        moved = fixed + (places - fixed + rotation * (used - fixed)) % max(1, count - fixed)
        return jnp.zeros((count,), jnp.int32).at[order[jnp.where(places < fixed, places, moved)]].set(jnp.asarray(sizes, jnp.int32))

    sizes = jnp.where(number % 4 == 0, named(packed, number // 4), named(common, number - number // 4 - 1))
    mixed = jax.random.permutation(jax.random.fold_in(own, 3), count)
    giver, taker = mixed[0:count // 2 * 2:2], mixed[1:count // 2 * 2:2]
    margin = jnp.minimum(sizes[giver] - 1, most - sizes[taker]) // 2
    margin = jnp.where((giver == order[0]) | (taker == order[0]) | (sizes[taker] == 0), 0, jnp.maximum(margin, 0))
    moved = jax.random.randint(jax.random.fold_in(own, 4), (count // 2,), 0, 1 << 20) % (margin + 1)
    sizes = sizes.at[giver].add(-moved).at[taker].add(moved)
    members = jnp.searchsorted(jnp.cumsum(sizes), jnp.arange(rows * top), side="right").astype(jnp.int32)
    table = members.reshape(top, rows).T
    table = table[jax.random.permutation(jax.random.fold_in(own, 1), rows)]
    rotation = jax.random.randint(jax.random.fold_in(own, 2), (rows, 1), 0, top)
    return jnp.take_along_axis(table, (jnp.arange(top)[None, :] + rotation) % top, axis=1)


def portions_of(number_of, total, bound, skew, full):
    loads = [(1 << 20) // math.isqrt(grade ** skew) + 1 for grade in range(1, number_of + 1)]
    largest = bound if full else min(bound, max(-(-total // number_of), total * loads[0] // sum(loads)))
    least = 1 if total - largest >= number_of - 1 else 0
    holding, spare = [largest] + [least] * (number_of - 1), total - largest - least * (number_of - 1)
    while spare > 0:
        movable = [i for i in range(1, number_of) if holding[i] < largest] or [i for i in range(1, number_of) if holding[i] < bound]
        pool, remaining = sum([loads[i] for i in movable]), spare
        for i in movable:
            addition = min(bound - holding[i], max(1, remaining * loads[i] // pool), spare)
            holding[i] = holding[i] + addition
            spare = spare - addition
    return np.array(holding)


def setup_inputs(seed: int = 0) -> dict:
    keys = jax.random.split(jax.random.key(seed), 8)
    probe_signs = set_ends((jax.random.randint(keys[0], (PROBES, DEVICES, TILES_DEV, FR, FC), 0, 2) < 1).astype(jnp.int32), jax.random.fold_in(keys[0], 1), 0, 1)
    trial_rows = set_ends(jax.random.randint(keys[1], (TRIALS,), 2 * FR + 1, FIELD_ROWS + 1), jax.random.fold_in(keys[1], 1), 2 * FR + 1, FIELD_ROWS).astype(jnp.int32)
    trial_cols = set_ends(jax.random.randint(keys[2], (TRIALS,), FC // 2, FC + 1), jax.random.fold_in(keys[2], 1), FC // 2, FC).astype(jnp.int32)
    ar_rho = jnp.clip(0.1 + 0.59999999 * jax.random.uniform(keys[3], (TRIALS, 2), jnp.float32) ** steps_of(keys[3], (TRIALS, 2), ((0, 8),), -0.2, 0.2), 0.1, 0.7)
    res_var = jnp.clip(jnp.exp(math.log(16.0) - 1.3862944 * jax.random.uniform(keys[4], (TRIALS,), jnp.float32) ** steps_of(keys[4], (TRIALS,), ((0, 8),), -0.2, 0.2)), 4.0, 16.0)
    plot_owner_keys = jax.random.split(jax.random.fold_in(keys[5], 1), DEVICES * TILES_DEV * FR * FC // P_DEV)
    plot_owner_turns = jax.random.permutation(jax.random.fold_in(keys[5], 3), DEVICES * TILES_DEV * FR * FC // P_DEV)
    plot_owner = jax.vmap(lambda own, number: shared_out(jax.random.fold_in(keys[5], 2), own, number, P_DEV, DEVICES, 1, CAP, 2))(plot_owner_keys, plot_owner_turns).reshape((DEVICES, TILES_DEV, FR, FC, 1))
    plot_slot = set_ends(jax.random.randint(keys[6], (DEVICES, TILES_DEV, FR, FC), 0, G_DEV), jax.random.fold_in(keys[6], 1), 0, G_DEV - 1).astype(jnp.int32)
    return {"probe_signs": probe_signs, "trial_rows": trial_rows, "trial_cols": trial_cols, "ar_rho": ar_rho, "res_var": res_var, "plot_owner": plot_owner, "plot_slot": plot_slot}


def line_coeffs(rho_vals, cell_count, positions):
    inverse = 1.0 / (1.0 - rho_vals * rho_vals)
    edge_mask = (positions[None, :] == 0) | (positions[None, :] == cell_count[:, None] - 1)
    inside = 1.0 + rho_vals * rho_vals
    main_diag = jnp.where(edge_mask, inverse[:, None], (inverse * inside)[:, None])
    main_slope = jnp.where(edge_mask, (2.0 * rho_vals * inverse * inverse)[:, None], (4.0 * rho_vals * inverse * inverse)[:, None])
    off_diag = -inverse * rho_vals
    off_slope = -inside * inverse * inverse
    return main_diag, off_diag, main_slope, off_slope


def across_columns(field_vals, main_diag, off_diag):
    padded = jnp.pad(field_vals, ((0, 0), (0, 0), (0, 0), (1, 1)))
    return main_diag[:, None, :] * field_vals + off_diag[:, None, None] * (padded[..., :-2] + padded[..., 2:])


def across_rows(padded, main_diag, off_diag):
    return main_diag[:, :, None] * padded[:, :, 1:-1, :] + off_diag[:, None, None] * (padded[:, :, :-2, :] + padded[:, :, 2:, :])


def reference(probe_signs, trial_rows, trial_cols, ar_rho, res_var, plot_owner, plot_slot):
    probe_count = probe_signs.shape[0]
    stacked = probe_signs.reshape(probe_count, N_TRIAL, N_GENO, TILES_DEV, FR, FC)
    stacked = stacked.transpose(0, 1, 3, 2, 4, 5).reshape(probe_count, TRIALS, FIELD_ROWS, FC)
    row_pos = jnp.arange(FIELD_ROWS, dtype=jnp.int32)
    col_pos = jnp.arange(FC, dtype=jnp.int32)
    present = (row_pos[None, :, None] < trial_rows[:, None, None]) & (col_pos[None, None, :] < trial_cols[:, None, None])
    probe_field = jnp.where(present[None], 2.0 * stacked.astype(jnp.float32) - 1.0, jnp.float32(0.0))
    col_diag, col_off, col_sdiag, col_soff = line_coeffs(ar_rho[:, 1], trial_cols, col_pos)
    row_diag, row_off, row_sdiag, row_soff = line_coeffs(ar_rho[:, 0], trial_rows, row_pos)
    col_field = across_columns(probe_field, col_diag, col_off)
    col_slope = across_columns(probe_field, col_sdiag, col_soff)
    plot_scale = jnp.where(present, (1.0 / res_var)[:, None, None], jnp.float32(0.0))
    pad_rows = ((0, 0), (0, 0), (1, 1), (0, 0))
    field_pad = jnp.pad(col_field, pad_rows)
    slope_pad = jnp.pad(col_slope, pad_rows)
    genotype = (plot_owner.reshape(-1) * G_DEV + plot_slot.reshape(-1)).astype(jnp.int32)
    results = []
    for image in (across_rows(field_pad, row_diag, row_off), across_rows(field_pad, row_sdiag, row_soff), across_rows(slope_pad, row_diag, row_off)):
        plot_terms = (image * plot_scale[None]).astype(jnp.bfloat16)
        flat_terms = plot_terms.reshape(probe_count, N_TRIAL, TILES_DEV, N_GENO, FR, FC)
        flat_terms = flat_terms.transpose(0, 1, 3, 2, 4, 5).reshape(probe_count, -1).astype(jnp.float32)
        summed = jax.ops.segment_sum(flat_terms.T, genotype, num_segments=G)
        results.append(summed.T)
    return jnp.stack(results, 0)
```

```python
import functools

import jax
import jax.numpy as jnp
from jax import lax
from jax.experimental import pallas as pl
from jax.experimental.pallas import tpu as pltpu
from jax.sharding import PartitionSpec as P

G_DEV = 1024
TILE = 16
CHUNK = 256
PAIR = 2


def round_up(value, step):
    return -(-value // step) * step


def line_coeffs(rho, cell_count, positions):
    inverse = 1.0 / (1.0 - rho * rho)
    edge_mask = (positions == 0) | (positions == cell_count - 1)
    inside = 1.0 + rho * rho
    main_diag = jnp.where(edge_mask, inverse, inverse * inside)
    main_slope = jnp.where(edge_mask, 2.0 * rho * inverse * inverse, 4.0 * rho * inverse * inverse)
    off_diag = -inverse * rho
    off_slope = -inside * inverse * inverse
    return main_diag, off_diag, main_slope, off_slope


def place_kernel(groups, bucket_tiles, group_ref, upper_ref, place_ref, tile_ref, count_ref, hot, cum):
    rows, cols = group_ref.shape
    blocks = rows // PAIR
    lanes = tile_ref.shape[1]
    group_id = lax.broadcasted_iota(jnp.int32, (groups, cols), 0)
    for row in range(rows):
        hot[row * groups : (row + 1) * groups, :] = (
            group_ref[row : row + 1, :] == group_id
        ).astype(jnp.float32)
    cum[...] = jnp.dot(
        hot[...].astype(jnp.bfloat16), upper_ref[...], preferred_element_type=jnp.float32
    )
    lane = lax.broadcasted_iota(jnp.int32, (groups, lanes), 1)
    counts = jnp.zeros((groups, lanes), jnp.float32)
    for block in range(blocks):
        total = jnp.zeros((groups, 1), jnp.float32)
        for row in range(block * PAIR, (block + 1) * PAIR):
            total = total + cum[row * groups : (row + 1) * groups, cols - 1 : cols]
        counts = jnp.where(lane == block, total, counts)
    tiles = jnp.floor((counts + (TILE - 1.0)) * (1.0 / TILE))
    before = (
        lax.broadcasted_iota(jnp.int32, (lanes, lanes), 0)
        < lax.broadcasted_iota(jnp.int32, (lanes, lanes), 1)
    ).astype(jnp.bfloat16)
    above = (
        lax.broadcasted_iota(jnp.int32, (groups, groups), 1)
        < lax.broadcasted_iota(jnp.int32, (groups, groups), 0)
    ).astype(jnp.bfloat16)
    tiles_bf = tiles.astype(jnp.bfloat16)
    earlier = jnp.dot(tiles_bf, before, preferred_element_type=jnp.float32)
    starts = jnp.dot(above, tiles_bf, preferred_element_type=jnp.float32)
    group_col = lax.broadcasted_iota(jnp.int32, (groups, lanes), 0).astype(jnp.float32)
    lane_f = lane.astype(jnp.float32)
    for block in range(blocks):
        start = starts[:, block : block + 1]
        number = tiles[:, block : block + 1]
        offset = start * float(TILE) - 1.0
        for row in range(block * PAIR, (block + 1) * PAIR):
            part = slice(row * groups, (row + 1) * groups)
            place_ref[row : row + 1, :] = jnp.sum(
                hot[part, :] * (cum[part, :] + offset), axis=0, keepdims=True
            ).astype(jnp.int32)
            offset = offset + cum[part, cols - 1 : cols]
        inside = (lane_f >= start) & (lane_f < start + number)
        goal = group_col * float(bucket_tiles) + earlier[:, block : block + 1] + lane_f - start
        chosen = jnp.sum(jnp.where(inside, goal + 1.0, 0.0), axis=0, keepdims=True)
        tile_ref[block : block + 1, :] = jnp.where(
            chosen > 0.0, chosen - 1.0, float(groups * bucket_tiles)
        ).astype(jnp.int32)
    count_ref[...] = earlier[:, blocks : blocks + 1].astype(jnp.int32) + jnp.zeros(
        (groups, lanes), jnp.int32
    )


def sums_kernel(
    groups,
    members,
    bucket_tiles,
    tile_ref,
    count_ref,
    field_ref,
    low_ref,
    high_ref,
    coef_ref,
    line_ref,
    member_ref,
    slot_ref,
    place_ref,
    send_ref,
    keep_ref,
    rows_all,
    bucket,
    acc,
):
    rows, probes, cols = field_ref.shape
    terms = 3 * probes
    stride = terms + TILE
    step = pl.program_id(0)
    blocks = rows // PAIR
    staged_tiles = PAIR * cols // TILE + groups
    staged = staged_tiles * TILE

    @pl.when(step == 0)
    def _():
        rows_all[0] = low_ref[...].astype(jnp.float32)
        rows_all[pl.ds(1, rows)] = field_ref[...]
        rows_all[rows + 1] = high_ref[...].astype(jnp.float32)
        col_pos = lax.broadcasted_iota(jnp.int32, (probes, cols), 1)
        col_diag, col_slope_diag = line_ref[0:1, :], line_ref[1:2, :]
        col_off, col_slope_off = line_ref[2:3, :], line_ref[3:4, :]
        row_off, row_slope_off = line_ref[4:5, :], line_ref[5:6, :]

        def sort_block(block, carry):
            first = block * PAIR
            values, slopes = [], []
            for row in range(PAIR + 2):
                cells = rows_all[first + row]
                beside = jnp.where(col_pos == 0, 0.0, pltpu.roll(cells, 1, 1)) + jnp.where(
                    col_pos == cols - 1, 0.0, pltpu.roll(cells, cols - 1, 1)
                )
                values.append(col_diag * cells + col_off * beside)
                slopes.append(col_slope_diag * cells + col_slope_off * beside)
            parts = []
            for row in range(PAIR):
                coef = coef_ref[first + row]
                row_diag, row_slope_diag, scale = coef[0:1, :], coef[1:2, :], coef[2:3, :]
                value_beside = values[row] + values[row + 2]
                slope_beside = slopes[row] + slopes[row + 2]
                three = jnp.concatenate(
                    [
                        (row_diag * values[row + 1] + row_off * value_beside) * scale,
                        (row_slope_diag * values[row + 1] + row_slope_off * value_beside) * scale,
                        (row_diag * slopes[row + 1] + row_off * slope_beside) * scale,
                    ],
                    axis=0,
                )
                member = member_ref[pl.ds(first + row, 1), :]
                slot = slot_ref[pl.ds(first + row, 1), :]
                code_row = lax.broadcasted_iota(jnp.int32, (TILE, cols), 0)
                code = jnp.where(
                    code_row == 0,
                    lax.shift_right_logical(slot, 5),
                    jnp.where(code_row == 1, lax.bitwise_and(slot, 31), 0),
                ).astype(jnp.float32)
                masked = []
                for index in range(members):
                    masked.append(jnp.where(member == index, three, 0.0))
                    masked.append(code)
                parts.append(jnp.concatenate(masked, axis=0).astype(jnp.bfloat16))
            payload = jnp.concatenate(parts, axis=1)
            place = jnp.concatenate(
                [place_ref[pl.ds(first + row, 1), :] for row in range(PAIR)], axis=1
            )
            chosen = (
                lax.broadcasted_iota(jnp.int32, (staged, PAIR * cols), 0) == place
            ).astype(jnp.bfloat16)
            ordered = lax.dot_general(
                chosen, payload, (((1,), (1,)), ((), ())), preferred_element_type=jnp.float32
            ).astype(jnp.bfloat16)
            for tile in range(staged_tiles):
                goal = pl.multiple_of(tile_ref[block, tile] * TILE, TILE)
                bucket[pl.ds(goal, TILE), :] = ordered[tile * TILE : (tile + 1) * TILE, :]
            return carry

        lax.fori_loop(0, blocks, sort_block, 0)

    used = count_ref[step, 0]
    base = step * (bucket_tiles * TILE)
    clear = jnp.zeros((TILE, members * stride), jnp.bfloat16)
    for tile in range(CHUNK // TILE):
        bucket[pl.ds(pl.multiple_of(base + (used + tile) * TILE, TILE), TILE), :] = clear
    acc[...] = jnp.zeros_like(acc)
    slot_lane = lax.broadcasted_iota(jnp.int32, (CHUNK, acc.shape[1]), 1)

    def add_chunk(chunk, carry):
        part = bucket[pl.ds(pl.multiple_of(base + chunk * CHUNK, CHUNK), CHUNK), :]
        code = part[:, terms : terms + 2].astype(jnp.float32)
        slot = (code[:, 0:1] * 32.0 + code[:, 1:2]).astype(jnp.int32)
        incidence = (slot == slot_lane).astype(jnp.bfloat16)
        acc[...] += lax.dot_general(
            part, incidence, (((0,), (0,)), ((), ())), preferred_element_type=jnp.float32
        )
        return carry

    lax.fori_loop(0, pl.cdiv(used * TILE, CHUNK), add_chunk, 0)
    for index in range(members):
        result = acc[index * stride : index * stride + terms, :]
        if index % 2:
            send_ref[index // 2, 0] = result.astype(jnp.bfloat16)
        else:
            keep_ref[index // 2, 0] = result


def exchange(block, axis, bit):
    count = lax.axis_size(axis)
    return lax.ppermute(block, axis, [(i, i ^ bit) for i in range(count)])


def body(probe_signs, trial_rows, trial_cols, ar_rho, res_var, plot_owner, plot_slot):
    signs = probe_signs.reshape(probe_signs.shape[0], *probe_signs.shape[3:])
    probes, rows, cols = signs.shape
    groups, members = lax.axis_size("trial"), lax.axis_size("geno")
    terms = 3 * probes
    stride = terms + TILE
    plots = rows * cols
    blocks = rows // PAIR
    band = lax.axis_index("geno")
    here = lax.axis_index("trial") * members + band
    row_pos = band * rows + jnp.arange(rows, dtype=jnp.int32)
    col_pos = jnp.arange(cols, dtype=jnp.int32)
    row_in, col_in = row_pos < trial_rows[0], col_pos < trial_cols[0]
    field = jnp.where(
        row_in[:, None, None] & col_in[None, None, :],
        2.0 * signs.transpose(1, 0, 2).astype(jnp.float32) - 1.0,
        jnp.float32(0.0),
    )

    def edge(row):
        return jnp.where(
            row_in[row] & col_in[None, :],
            2.0 * signs[:, row, :].astype(jnp.float32) - 1.0,
            jnp.float32(0.0),
        ).astype(jnp.bfloat16)

    up = [(i, i + 1) for i in range(members - 1)]
    low = lax.ppermute(edge(rows - 1), "geno", up)
    high = lax.ppermute(edge(0), "geno", [(j, i) for i, j in up])

    col_diag, col_off, col_sdiag, col_soff = line_coeffs(ar_rho[0, 1], trial_cols[0], col_pos)
    row_diag, row_off, row_sdiag, row_soff = line_coeffs(ar_rho[0, 0], trial_rows[0], row_pos)
    scale = jnp.where(row_in[:, None] & col_in[None, :], 1.0 / res_var[0], jnp.float32(0.0))
    wide = jnp.zeros((rows, cols), jnp.float32)
    coef = jnp.stack([row_diag[:, None] + wide, row_sdiag[:, None] + wide, scale], axis=1)
    flat = jnp.zeros((cols,), jnp.float32)
    line = jnp.stack(
        [col_diag, col_sdiag, col_off + flat, col_soff + flat, row_off + flat, row_soff + flat]
    )

    owner = plot_owner.reshape(rows, cols) ^ here
    group, member = owner // members, owner % members
    slot = plot_slot.reshape(rows, cols)

    group_rows = round_up(groups, 8)
    capacity = min(plots, members * max(1, 2 * plots // (groups * members)))
    bucket_tiles = (round_up(capacity + blocks * (TILE - 1), CHUNK) + CHUNK) // TILE
    lanes = 128
    assert PAIR * cols // TILE + group_rows <= lanes and blocks < lanes
    upper = (
        jnp.arange(cols, dtype=jnp.int32)[:, None] <= jnp.arange(cols, dtype=jnp.int32)[None, :]
    ).astype(jnp.bfloat16)
    vmem = pl.BlockSpec(memory_space=pltpu.VMEM)
    place, tile, count = pl.pallas_call(
        functools.partial(place_kernel, group_rows, bucket_tiles),
        out_shape=[
            jax.ShapeDtypeStruct((rows, cols), jnp.int32),
            jax.ShapeDtypeStruct((blocks, lanes), jnp.int32),
            jax.ShapeDtypeStruct((group_rows, lanes), jnp.int32),
        ],
        in_specs=[vmem, vmem],
        out_specs=[vmem, vmem, vmem],
        scratch_shapes=[
            pltpu.VMEM((rows * group_rows, cols), jnp.float32),
            pltpu.VMEM((rows * group_rows, cols), jnp.float32),
        ],
        name="place_plots",
    )(group, upper)

    smem = pl.BlockSpec(memory_space=pltpu.SMEM)
    half = members // 2
    send, keep = pl.pallas_call(
        functools.partial(sums_kernel, group_rows, members, bucket_tiles),
        grid=(groups,),
        out_shape=[
            jax.ShapeDtypeStruct((half, groups, terms, G_DEV), jnp.bfloat16),
            jax.ShapeDtypeStruct((half, groups, terms, G_DEV), jnp.float32),
        ],
        in_specs=[smem, smem] + [vmem] * 8,
        out_specs=[
            pl.BlockSpec((half, 1, terms, G_DEV), lambda i: (0, i, 0, 0)),
            pl.BlockSpec((half, 1, terms, G_DEV), lambda i: (0, i, 0, 0)),
        ],
        scratch_shapes=[
            pltpu.VMEM((rows + 2, probes, cols), jnp.float32),
            pltpu.VMEM(((group_rows * bucket_tiles + 1) * TILE, members * stride), jnp.bfloat16),
            pltpu.VMEM((members * stride, G_DEV), jnp.float32),
        ],
        compiler_params=pltpu.CompilerParams(vmem_limit_bytes=56 * 1024 * 1024),
        name="sum_plots",
    )(tile, count, field, low, high, coef, line, member, slot, place)

    received = exchange(send, "geno", 1)
    dims = [("geno", 1 << i) for i in range(1, members.bit_length() - 1)]
    dims += [("trial", 1 << i) for i in range(groups.bit_length() - 1)]
    shape = [2] * len(dims)
    geno_bits = members.bit_length() - 2
    trial_bits = groups.bit_length() - 1
    names = [("geno", 1 << (i + 1)) for i in reversed(range(geno_bits))]
    names += [("trial", 1 << i) for i in reversed(range(trial_bits))]
    keep = keep.reshape(shape + [3, probes, G_DEV])
    received = received.reshape(shape + [3, probes, G_DEV])
    outs = []
    for part in range(3):
        order = list(dims)
        lead = order.pop(part % len(order))
        order = [lead] + order
        total = keep[..., part, :, :] + received[..., part, :, :].astype(jnp.float32)
        left = list(names)
        for name in order:
            at = left.index(name)
            mine = lax.index_in_dim(total, 0, at, keepdims=False)
            other = lax.index_in_dim(total, 1, at, keepdims=False)
            if len(left) > 1:
                other = other.astype(jnp.bfloat16)
            total = mine + exchange(other, *name).astype(jnp.float32)
            left.remove(name)
        outs.append(total)
    return jnp.stack(outs, 0)


def solution(mesh):
    return jax.shard_map(
        body,
        mesh=mesh,
        in_specs=(
            P(None, ("trial", "geno"), None, None, None),
            P("trial"),
            P("trial"),
            P("trial", None),
            P("trial"),
            P(("trial", "geno"), None, None, None, None),
            P(("trial", "geno"), None, None, None),
        ),
        out_specs=P(None, None, ("trial", "geno")),
        check_vma=False,
    )
```

```python
import functools
import math

import jax
import jax.numpy as jnp
from jax import lax
from jax.experimental import pallas as pl
from jax.experimental.pallas import tpu as pltpu
from jax.sharding import PartitionSpec as P

G_DEV = 1024
TILE = 16
CHUNK = 512
BLOCK = 4
LANES = 128
HALVES = 2
OWNERS = 2
MEMBERS = HALVES * OWNERS
UNROLL = 11
TOGETHER = 4
CODE = 32


def round_up(value, step):
    return -(-value // step) * step


def signs_to_field(signs, row_in, col_in):
    return jnp.where(row_in & col_in, 2.0 * signs.astype(jnp.float32) - 1.0, 0.0)


def edge_kernel(size_ref, cols_ref, first_ref, last_ref, up_ref, down_ref):
    parts = up_ref.shape[1] // LANES
    rows = size_ref[2]
    lane = lax.broadcasted_iota(jnp.int32, (up_ref.shape[0], LANES), 1)
    for part in range(parts):
        col_in = lane + part * LANES < cols_ref[0]
        here = slice(part * LANES, (part + 1) * LANES)
        last = last_ref[:, last_ref.shape[1] - parts + part, :]
        up_ref[:, here] = signs_to_field(last, size_ref[1] + rows - 1 < size_ref[0], col_in).astype(
            jnp.bfloat16
        )
        first = first_ref[:, part, :]
        down_ref[:, here] = signs_to_field(first, size_ref[1] < size_ref[0], col_in).astype(
            jnp.bfloat16
        )


def prepare_kernel(
    groups,
    trash_tile,
    size_ref,
    cols_ref,
    rho_ref,
    var_ref,
    signs_ref,
    owner_ref,
    slot_ref,
    field_ref,
    line_ref,
    member_ref,
    place_ref,
    table_ref,
    hot,
    cum,
):
    rows, probes, cols = field_ref.shape
    parts = cols // LANES
    segments = rows * parts
    blocks = segments // BLOCK
    for part in range(parts):
        col_in = (
            lax.broadcasted_iota(jnp.int32, (probes, LANES), 1) + part * LANES < cols_ref[0]
        )
        for row in range(rows):
            field_ref[row, :, part * LANES : (part + 1) * LANES] = signs_to_field(
                signs_ref[:, row * parts + part, :], size_ref[1] + row < size_ref[0], col_in
            )
    pos = lax.broadcasted_iota(jnp.int32, (1, cols), 1)
    flat = jnp.zeros((1, cols), jnp.float32)
    rho = flat + rho_ref[0, 1]
    inverse = 1.0 / (1.0 - rho * rho)
    inside = 1.0 + rho * rho
    edge = (pos == 0) | (pos == cols_ref[0] - 1)
    line_ref[0:1, :] = jnp.where(edge, inverse, inverse * inside)
    line_ref[1:2, :] = jnp.where(
        edge, 2.0 * rho * inverse * inverse, 4.0 * rho * inverse * inverse
    )
    line_ref[2:3, :] = -inverse * rho
    line_ref[3:4, :] = -inside * inverse * inverse
    rho = flat + rho_ref[0, 0]
    inverse = 1.0 / (1.0 - rho * rho)
    inside = 1.0 + rho * rho
    line_ref[4:5, :] = -inverse * rho
    line_ref[5:6, :] = -inside * inverse * inverse
    line_ref[6:7, :] = inverse
    line_ref[7:8, :] = inverse * inside
    line_ref[8:9, :] = 2.0 * rho * inverse * inverse
    line_ref[9:10, :] = 4.0 * rho * inverse * inverse
    line_ref[10:11, :] = jnp.where(pos < cols_ref[0], 1.0 / (flat + var_ref[0]), 0.0)
    owner = jnp.bitwise_xor(owner_ref[...], size_ref[3])
    rest = lax.shift_right_logical(owner, 1)
    group_of = lax.shift_right_logical(rest, 1) + jnp.where(
        jnp.bitwise_and(owner, 1) == 1, 0, size_ref[4]
    )
    slot = slot_ref[...]
    member_ref[...] = jnp.bitwise_and(rest, 1) * HALVES + jnp.where(
        slot >= G_DEV // HALVES, 1, 0
    )
    group_id = lax.broadcasted_iota(jnp.int32, (groups, LANES), 0)
    for seg in range(segments):
        hot[seg * groups : (seg + 1) * groups, :] = (
            group_of[seg : seg + 1, :] == group_id
        ).astype(jnp.float32)
    square = (LANES, LANES)
    upper = lax.broadcasted_iota(jnp.int32, square, 0) <= lax.broadcasted_iota(jnp.int32, square, 1)
    before = lax.broadcasted_iota(jnp.int32, square, 0) < lax.broadcasted_iota(jnp.int32, square, 1)
    cum[...] = jnp.dot(
        hot[...].astype(jnp.bfloat16),
        upper.astype(jnp.bfloat16),
        preferred_element_type=jnp.float32,
    )
    lane = lax.broadcasted_iota(jnp.int32, (groups, LANES), 1)
    counts = jnp.zeros((groups, LANES), jnp.float32)
    for block in range(blocks):
        total = jnp.zeros((groups, 1), jnp.float32)
        for seg in range(block * BLOCK, (block + 1) * BLOCK):
            total = total + cum[seg * groups : (seg + 1) * groups, LANES - 1 : LANES]
        counts = jnp.where(lane == block, total, counts)
    tiles = jnp.floor((counts + (TILE - 1.0)) * (1.0 / TILE))
    above = (
        lax.broadcasted_iota(jnp.int32, (groups, groups), 1)
        < lax.broadcasted_iota(jnp.int32, (groups, groups), 0)
    ).astype(jnp.bfloat16)
    tiles_bf = tiles.astype(jnp.bfloat16)
    earlier = jnp.dot(tiles_bf, before.astype(jnp.bfloat16), preferred_element_type=jnp.float32)
    starts = jnp.dot(above, tiles_bf, preferred_element_type=jnp.float32)
    base = jnp.sum(starts, axis=1, keepdims=True)
    lane_f = lane.astype(jnp.float32)
    for block in range(blocks):
        start = starts[:, block : block + 1]
        number = tiles[:, block : block + 1]
        offset = start * float(TILE) - 1.0
        for seg in range(block * BLOCK, (block + 1) * BLOCK):
            here = slice(seg * groups, (seg + 1) * groups)
            place_ref[seg : seg + 1, :] = jnp.sum(
                hot[here, :] * (cum[here, :] + offset), axis=0, keepdims=True
            ).astype(jnp.int32)
            offset = offset + cum[here, LANES - 1 : LANES]
        held = (lane_f >= start) & (lane_f < start + number)
        goal = base + earlier[:, block : block + 1] + lane_f - start
        chosen = jnp.sum(jnp.where(held, goal + 1.0, 0.0), axis=0, keepdims=True)
        table_ref[block : block + 1, :] = jnp.where(
            chosen > 0.0, chosen - 1.0, float(trash_tile)
        ).astype(jnp.int32)
    total = earlier[:, blocks : blocks + 1]
    step = float(CHUNK // TILE)
    chunks = jnp.floor((total + (step - 1.0)) * (1.0 / step))
    group_row = lax.broadcasted_iota(jnp.int32, (groups, LANES), 0)
    ends = []
    for half in range(2):
        mine = (group_row >= half * (groups // 2)) & (group_row < (half + 1) * (groups // 2))
        own = jnp.where(mine, chunks, 0.0)
        first = jnp.dot(above, own.astype(jnp.bfloat16), preferred_element_type=jnp.float32)
        held = mine & (lane_f >= first) & (lane_f < first + own)
        index = lane_f - first
        fields = (
            base + step * index,
            (total - step * index) * float(TILE),
            (group_row - half * (groups // 2)).astype(jnp.float32),
        )
        for row, value in enumerate(fields):
            at = blocks + 3 * half + row
            table_ref[at : at + 1, :] = jnp.sum(
                jnp.where(held, value, 0.0), axis=0, keepdims=True
            ).astype(jnp.int32)
        ends.append(jnp.sum(own, axis=0, keepdims=True))
    every = jnp.sum(total + jnp.zeros((groups, LANES), jnp.float32), axis=0, keepdims=True)
    lane_row = lax.broadcasted_iota(jnp.int32, (1, LANES), 1)
    table_ref[blocks + 6 : blocks + 7, :] = jnp.where(
        lane_row == 0, ends[0], jnp.where(lane_row == 1, ends[1], every)
    ).astype(jnp.int32)


def sum_groups(half, blocks, terms, table_ref, bucket, acc, store):
    stride = terms + TILE
    acc[...] = jnp.zeros_like(acc)
    lane = lax.broadcasted_iota(jnp.int32, (LANES, LANES), 1)
    row_lane = lax.broadcasted_iota(jnp.int32, (1, CHUNK), 1)
    fold = LANES // stride

    def add_chunk(chunk):
        start = pl.multiple_of(table_ref[blocks + 3 * half, chunk] * TILE, TILE)
        left = table_ref[blocks + 3 * half + 1, chunk]
        group = table_ref[blocks + 3 * half + 2, chunk]
        part = bucket[pl.ds(start, CHUNK), :]
        codes = jnp.zeros((LANES, LANES), jnp.float32)
        spots = [(run % fold) * stride + terms + 2 * (run // fold) for run in range(CHUNK // LANES)]
        for run, spot in enumerate(spots):
            held = part[run * LANES : (run + 1) * LANES, 0:LANES].astype(jnp.float32)
            codes = jnp.where((lane == spot) | (lane == spot + 1), held, codes)
        codes = codes.T
        slot = jnp.concatenate(
            [codes[spot : spot + 1, :] * float(CODE) + codes[spot + 1 : spot + 2, :] for spot in spots],
            axis=1,
        ).astype(jnp.int32)
        slot = jnp.where(row_lane < left, slot, -1)
        incidence = (
            lax.broadcasted_iota(jnp.int32, (acc.shape[1], CHUNK), 0) == slot
        ).astype(jnp.bfloat16)
        acc[group] += jnp.dot(incidence, part, preferred_element_type=jnp.float32)

    def add_some(index, carry):
        for each in range(TOGETHER):
            add_chunk(index * TOGETHER + each)
        return carry

    number = table_ref[blocks + 6, half]
    lax.fori_loop(0, (number + TOGETHER - 1) // TOGETHER, add_some, 0)
    width = acc.shape[1]

    def finish(group, carry):
        result = acc[group].astype(store.dtype).T
        for index in range(MEMBERS):
            store[
                index // HALVES, group, :, (index % HALVES) * width : (index % HALVES + 1) * width
            ] = result[index * stride : index * stride + terms, :]
        return carry

    lax.fori_loop(0, acc.shape[0], finish, 0, unroll=2)


def sort_kernel(
    groups,
    size_ref,
    table_ref,
    field_ref,
    low_ref,
    high_ref,
    line_ref,
    member_ref,
    slot_ref,
    place_ref,
    send_ref,
    bucket,
    rows_all,
    acc,
):
    rows, probes, cols = field_ref.shape
    parts = cols // LANES
    pair = BLOCK // parts
    terms = 3 * probes
    stride = terms + TILE
    blocks = rows // pair
    staged_tiles = BLOCK * LANES // TILE + groups
    staged = staged_tiles * TILE

    rows_all[0] = low_ref[...].astype(jnp.float32)
    rows_all[pl.ds(1, rows)] = field_ref[...]
    rows_all[rows + 1] = high_ref[...].astype(jnp.float32)
    col_pos = lax.broadcasted_iota(jnp.int32, (probes, cols), 1)

    def sort_block(block, carry):
        first = block * pair
        values, slopes = [], []
        for row in range(pair + 2):
            cells = rows_all[first + row]
            beside = jnp.where(col_pos == 0, 0.0, pltpu.roll(cells, 1, 1)) + jnp.where(
                col_pos == cols - 1, 0.0, pltpu.roll(cells, cols - 1, 1)
            )
            values.append(line_ref[0:1, :] * cells + line_ref[2:3, :] * beside)
            slopes.append(line_ref[1:2, :] * cells + line_ref[3:4, :] * beside)

        def segment(ref, row):
            at = first * parts + row * parts
            return jnp.concatenate(
                [ref[pl.ds(at + part, 1), :] for part in range(parts)], axis=1
            )

        blocks_of = []
        for row in range(pair):
            pos = size_ref[1] + first + row
            edge = (pos == 0) | (pos == size_ref[0] - 1)
            row_diag = jnp.where(edge, line_ref[6:7, :], line_ref[7:8, :])
            row_slope_diag = jnp.where(edge, line_ref[8:9, :], line_ref[9:10, :])
            scale = jnp.where(pos < size_ref[0], line_ref[10:11, :], 0.0)
            row_off, row_slope_off = line_ref[4:5, :], line_ref[5:6, :]
            value_beside = values[row] + values[row + 2]
            slope_beside = slopes[row] + slopes[row + 2]
            three = jnp.concatenate(
                [
                    (row_diag * values[row + 1] + row_off * value_beside) * scale,
                    (row_slope_diag * values[row + 1] + row_slope_off * value_beside) * scale,
                    (row_diag * slopes[row + 1] + row_off * slope_beside) * scale,
                ],
                axis=0,
            )
            member = segment(member_ref, row)
            slot = jnp.bitwise_and(segment(slot_ref, row), G_DEV // HALVES - 1)
            code_row = lax.broadcasted_iota(jnp.int32, (TILE, cols), 0)
            code = jnp.where(
                jnp.bitwise_and(code_row, 1) == 0, lax.div(slot, CODE), lax.rem(slot, CODE)
            ).astype(jnp.float32)
            masked = []
            for index in range(MEMBERS):
                masked.append(jnp.where(member == index, three, 0.0))
                masked.append(code)
            blocks_of.append(jnp.concatenate(masked, axis=0).astype(jnp.bfloat16))
        payload = jnp.concatenate(blocks_of, axis=1)
        place = jnp.concatenate([segment(place_ref, row) for row in range(pair)], axis=1)
        chosen = (
            lax.broadcasted_iota(jnp.int32, (staged, BLOCK * LANES), 0) == place
        ).astype(jnp.bfloat16)
        ordered = lax.dot_general(
            chosen, payload, (((1,), (1,)), ((), ())), preferred_element_type=jnp.float32
        ).astype(jnp.bfloat16)
        for tile in range(staged_tiles):
            goal = pl.multiple_of(table_ref[block, tile] * TILE, TILE)
            bucket[pl.ds(goal, TILE), :] = ordered[tile * TILE : (tile + 1) * TILE, :]
        return carry

    lax.fori_loop(0, blocks, sort_block, 0, unroll=UNROLL)
    end = table_ref[blocks + 6, 2]
    clear = jnp.zeros((TILE, bucket.shape[1]), jnp.bfloat16)
    for tile in range(CHUNK // TILE):
        bucket[pl.ds(pl.multiple_of((end + tile) * TILE, TILE), TILE), :] = clear
    sum_groups(0, blocks, terms, table_ref, bucket, acc, send_ref)


def keep_kernel(blocks, table_ref, bucket, keep_ref, acc):
    sum_groups(1, blocks, keep_ref.shape[2], table_ref, bucket, acc, keep_ref)


def exchange(block, axis, bit):
    count = lax.axis_size(axis)
    return lax.ppermute(block, axis, [(i, i ^ bit) for i in range(count)])


def body(probe_signs, trial_rows, trial_cols, ar_rho, res_var, plot_owner, plot_slot):
    probes, rows, cols = probe_signs.shape[0], probe_signs.shape[3], probe_signs.shape[4]
    trials, bands = lax.axis_size("trial"), lax.axis_size("geno")
    devices = trials * bands
    terms = 3 * probes
    stride = terms + TILE
    plots = rows * cols
    segments = plots // LANES
    blocks = segments // BLOCK
    groups = devices // OWNERS
    band = lax.axis_index("geno")
    here = lax.axis_index("trial") * bands + band
    size = jnp.stack(
        [
            trial_rows[0],
            band * rows,
            jnp.int32(rows),
            here,
            jnp.int32(groups // 2),
        ]
    ).astype(jnp.int32)
    signs = probe_signs.reshape(probes, segments, LANES)
    vmem = pl.BlockSpec(memory_space=pltpu.VMEM)
    smem = pl.BlockSpec(memory_space=pltpu.SMEM)

    edge_shape = jax.ShapeDtypeStruct((probes, cols), jnp.bfloat16)
    tail = segments // 8 - 1
    up_row, down_row = pl.pallas_call(
        edge_kernel,
        grid=(1,),
        out_shape=[edge_shape, edge_shape],
        in_specs=[
            smem,
            smem,
            pl.BlockSpec((probes, 8, LANES), lambda i: (0, 0, 0)),
            pl.BlockSpec((probes, 8, LANES), lambda i: (0, tail, 0)),
        ],
        out_specs=[pl.BlockSpec((probes, cols), lambda i: (0, 0))] * 2,
        name="edge_rows",
    )(size, trial_cols, signs, signs)
    up = [(i, i + 1) for i in range(bands - 1)]
    low = lax.ppermute(up_row, "geno", up)
    high = lax.ppermute(down_row, "geno", [(j, i) for i, j in up])

    assert BLOCK * LANES // TILE + groups <= LANES and blocks < LANES
    assert plots // CHUNK + groups // 2 + TOGETHER <= LANES
    tiles = blocks * (BLOCK * LANES // TILE + groups)
    trash_tile = tiles + CHUNK // TILE
    bucket_shape = ((trash_tile + 1) * TILE, MEMBERS * stride)
    half = groups // 2
    acc_shape = (half, G_DEV // HALVES, MEMBERS * stride)
    out_shape = (OWNERS, half, terms, G_DEV)
    mib = 1024 * 1024
    bucket_bytes, acc_bytes = 2 * math.prod(bucket_shape), 4 * math.prod(acc_shape)
    segs = jax.ShapeDtypeStruct((segments, LANES), jnp.int32)
    slot = plot_slot.reshape(segments, LANES)
    field, line, member, place, table = pl.pallas_call(
        functools.partial(prepare_kernel, groups, trash_tile),
        out_shape=[
            jax.ShapeDtypeStruct((rows, probes, cols), jnp.float32),
            jax.ShapeDtypeStruct((16, cols), jnp.float32),
            segs,
            segs,
            jax.ShapeDtypeStruct((blocks + 8, LANES), jnp.int32),
        ],
        in_specs=[smem] * 4 + [vmem] * 3,
        out_specs=[vmem] * 5,
        scratch_shapes=[
            pltpu.VMEM((segments * groups, LANES), jnp.float32),
            pltpu.VMEM((segments * groups, LANES), jnp.float32),
        ],
        compiler_params=pltpu.CompilerParams(vmem_limit_bytes=12 * mib),
        name="prepare_plots",
    )(size, trial_cols, ar_rho, res_var, signs, plot_owner.reshape(segments, LANES), slot)

    send, bucket = pl.pallas_call(
        functools.partial(sort_kernel, groups),
        out_shape=[
            jax.ShapeDtypeStruct(out_shape, jnp.bfloat16),
            jax.ShapeDtypeStruct(bucket_shape, jnp.bfloat16),
        ],
        in_specs=[smem] * 2 + [vmem] * 7,
        out_specs=[vmem] * 2,
        scratch_shapes=[
            pltpu.VMEM((rows + 2, probes, cols), jnp.float32),
            pltpu.VMEM(acc_shape, jnp.float32),
        ],
        compiler_params=pltpu.CompilerParams(
            vmem_limit_bytes=bucket_bytes + acc_bytes + 2 * math.prod(out_shape) + 10 * mib
        ),
        name="sort_plots",
    )(size, table, field, low, high, line, member, slot, place)
    received = exchange(send, "geno", 1)
    keep = pl.pallas_call(
        functools.partial(keep_kernel, blocks),
        out_shape=jax.ShapeDtypeStruct(out_shape, jnp.float32),
        in_specs=[smem, vmem],
        out_specs=vmem,
        scratch_shapes=[pltpu.VMEM(acc_shape, jnp.float32)],
        compiler_params=pltpu.CompilerParams(
            vmem_limit_bytes=bucket_bytes + acc_bytes + 4 * math.prod(out_shape) + 6 * mib
        ),
        cost_estimate=pl.CostEstimate(
            flops=2 * plots * MEMBERS * stride * G_DEV // HALVES, bytes_accessed=bucket_bytes, transcendentals=0
        ),
        name="sum_kept",
    )(table, bucket)
    geno_bits, trial_bits = bands.bit_length() - 1, trials.bit_length() - 1
    names = [("geno", 2)]
    names += [("trial", 1 << i) for i in reversed(range(trial_bits))]
    names += [("geno", 1 << i) for i in reversed(range(2, geno_bits))]
    dims = [("geno", 2)] + [("trial", 1 << i) for i in range(trial_bits)]
    dims += [("geno", 1 << i) for i in range(2, geno_bits)]
    shape = [2] * len(dims)
    keep = keep.reshape(shape + [3, probes, G_DEV])
    received = received.reshape(shape + [3, probes, G_DEV])
    outs = []
    for part in range(3):
        order = list(dims)
        order = [order.pop(part % len(order))] + order
        total = keep[..., part, :, :] + received[..., part, :, :].astype(jnp.float32)
        left = list(names)
        for name in order:
            at = left.index(name)
            mine = lax.index_in_dim(total, 0, at, keepdims=False)
            other = lax.index_in_dim(total, 1, at, keepdims=False)
            if len(left) > 1:
                other = other.astype(jnp.bfloat16)
            total = mine + exchange(other, *name).astype(jnp.float32)
            left.remove(name)
        outs.append(total)
    return jnp.stack(outs, 0)


def solution(mesh):
    return jax.shard_map(
        body,
        mesh=mesh,
        in_specs=(
            P(None, ("trial", "geno"), None, None, None),
            P("trial"),
            P("trial"),
            P("trial", None),
            P("trial"),
            P(("trial", "geno"), None, None, None, None),
            P(("trial", "geno"), None, None, None),
        ),
        out_specs=P(None, None, ("trial", "geno")),
        check_vma=False,
    )
```

```python
import functools
import math

import jax
import jax.numpy as jnp
from jax import lax
from jax.experimental import pallas as pl
from jax.experimental.pallas import tpu as pltpu
from jax.sharding import PartitionSpec as P

G_DEV = 1024
TILE = 16
CHUNK = 512
BLOCK = 4
LANES = 128
HALVES = 2
OWNERS = 2
MEMBERS = HALVES * OWNERS
UNROLL = 11
TOGETHER = 4
CODE = 32


def round_up(value, step):
    return -(-value // step) * step


def bits_to_field(bits, row_in, col_in):
    return jnp.where(row_in & col_in, 2.0 * bits.astype(jnp.float32) - 1.0, 0.0)


def prepare(
    groups,
    trash_tile,
    size_ref,
    cols_ref,
    rho_ref,
    var_ref,
    signs_ref,
    low_ref,
    high_ref,
    genotype_ref,
    field_ref,
    line_ref,
    member_ref,
    place_ref,
    table_ref,
    hot,
    cum,
):
    rows, probes, cols = field_ref.shape[0] - 2, field_ref.shape[1], field_ref.shape[2]
    parts = cols // LANES
    segments = rows * parts
    blocks = segments // BLOCK
    for part in range(parts):
        col_in = (
            lax.broadcasted_iota(jnp.int32, (probes, LANES), 1) + part * LANES < cols_ref[0]
        )
        here = slice(part * LANES, (part + 1) * LANES)
        for row in range(rows):
            field_ref[row + 1, :, here] = jnp.where(
                (size_ref[1] + row < size_ref[0]) & col_in, signs_ref[:, row * parts + part, :], 0.0
            )
        field_ref[0, :, here] = bits_to_field(
            low_ref[:, part, :], (size_ref[1] > 0) & (size_ref[1] <= size_ref[0]), col_in
        )
        field_ref[rows + 1, :, here] = bits_to_field(
            high_ref[:, part, :], size_ref[1] + rows < size_ref[0], col_in
        )
    pos = lax.broadcasted_iota(jnp.int32, (1, cols), 1)
    flat = jnp.zeros((1, cols), jnp.float32)
    rho = flat + rho_ref[0, 1]
    inverse = 1.0 / (1.0 - rho * rho)
    inside = 1.0 + rho * rho
    edge = (pos == 0) | (pos == cols_ref[0] - 1)
    line_ref[0:1, :] = jnp.where(edge, inverse, inverse * inside)
    line_ref[1:2, :] = jnp.where(
        edge, 2.0 * rho * inverse * inverse, 4.0 * rho * inverse * inverse
    )
    line_ref[2:3, :] = -inverse * rho
    line_ref[3:4, :] = -inside * inverse * inverse
    rho = flat + rho_ref[0, 0]
    inverse = 1.0 / (1.0 - rho * rho)
    inside = 1.0 + rho * rho
    line_ref[4:5, :] = -inverse * rho
    line_ref[5:6, :] = -inside * inverse * inverse
    line_ref[6:7, :] = inverse
    line_ref[7:8, :] = inverse * inside
    line_ref[8:9, :] = 2.0 * rho * inverse * inverse
    line_ref[9:10, :] = 4.0 * rho * inverse * inverse
    line_ref[10:11, :] = jnp.where(pos < cols_ref[0], 1.0 / (flat + var_ref[0]), 0.0)
    owner = lax.div(genotype_ref[...], G_DEV)
    rest = lax.shift_right_logical(owner, 1)
    group_of = lax.shift_right_logical(rest, 1) + jnp.where(
        jnp.bitwise_and(owner, 1) == 1, 0, size_ref[3]
    )
    slot = jnp.bitwise_and(genotype_ref[...], G_DEV - 1)
    member_ref[...] = jnp.bitwise_and(rest, 1) * HALVES + jnp.where(
        slot >= G_DEV // HALVES, 1, 0
    )
    group_id = lax.broadcasted_iota(jnp.int32, (groups, LANES), 0)
    for seg in range(segments):
        hot[seg * groups : (seg + 1) * groups, :] = (
            group_of[seg : seg + 1, :] == group_id
        ).astype(jnp.float32)
    square = (LANES, LANES)
    upper = lax.broadcasted_iota(jnp.int32, square, 0) <= lax.broadcasted_iota(jnp.int32, square, 1)
    before = lax.broadcasted_iota(jnp.int32, square, 0) < lax.broadcasted_iota(jnp.int32, square, 1)
    cum[...] = jnp.dot(
        hot[...].astype(jnp.bfloat16),
        upper.astype(jnp.bfloat16),
        preferred_element_type=jnp.float32,
    )
    lane = lax.broadcasted_iota(jnp.int32, (groups, LANES), 1)
    counts = jnp.zeros((groups, LANES), jnp.float32)
    for block in range(blocks):
        total = jnp.zeros((groups, 1), jnp.float32)
        for seg in range(block * BLOCK, (block + 1) * BLOCK):
            total = total + cum[seg * groups : (seg + 1) * groups, LANES - 1 : LANES]
        counts = jnp.where(lane == block, total, counts)
    tiles = jnp.floor((counts + (TILE - 1.0)) * (1.0 / TILE))
    above = (
        lax.broadcasted_iota(jnp.int32, (groups, groups), 1)
        < lax.broadcasted_iota(jnp.int32, (groups, groups), 0)
    ).astype(jnp.bfloat16)
    tiles_bf = tiles.astype(jnp.bfloat16)
    earlier = jnp.dot(tiles_bf, before.astype(jnp.bfloat16), preferred_element_type=jnp.float32)
    starts = jnp.dot(above, tiles_bf, preferred_element_type=jnp.float32)
    base = jnp.sum(starts, axis=1, keepdims=True)
    lane_f = lane.astype(jnp.float32)
    for block in range(blocks):
        start = starts[:, block : block + 1]
        number = tiles[:, block : block + 1]
        offset = start * float(TILE) - 1.0
        for seg in range(block * BLOCK, (block + 1) * BLOCK):
            here = slice(seg * groups, (seg + 1) * groups)
            place_ref[seg : seg + 1, :] = jnp.sum(
                hot[here, :] * (cum[here, :] + offset), axis=0, keepdims=True
            ).astype(jnp.int32)
            offset = offset + cum[here, LANES - 1 : LANES]
        held = (lane_f >= start) & (lane_f < start + number)
        goal = base + earlier[:, block : block + 1] + lane_f - start
        chosen = jnp.sum(jnp.where(held, goal + 1.0, 0.0), axis=0, keepdims=True)
        table_ref[block : block + 1, :] = jnp.where(
            chosen > 0.0, chosen - 1.0, float(trash_tile)
        ).astype(jnp.int32)
    total = earlier[:, blocks : blocks + 1]
    step = float(CHUNK // TILE)
    chunks = jnp.floor((total + (step - 1.0)) * (1.0 / step))
    group_row = lax.broadcasted_iota(jnp.int32, (groups, LANES), 0)
    ends = []
    for half in range(2):
        mine = (group_row >= half * (groups // 2)) & (group_row < (half + 1) * (groups // 2))
        own = jnp.where(mine, chunks, 0.0)
        first = jnp.dot(above, own.astype(jnp.bfloat16), preferred_element_type=jnp.float32)
        held = mine & (lane_f >= first) & (lane_f < first + own)
        index = lane_f - first
        fields = (
            base + step * index,
            (total - step * index) * float(TILE),
            (group_row - half * (groups // 2)).astype(jnp.float32),
        )
        for row, value in enumerate(fields):
            at = blocks + 3 * half + row
            table_ref[at : at + 1, :] = jnp.sum(
                jnp.where(held, value, 0.0), axis=0, keepdims=True
            ).astype(jnp.int32)
        ends.append(jnp.sum(own, axis=0, keepdims=True))
    every = jnp.sum(total + jnp.zeros((groups, LANES), jnp.float32), axis=0, keepdims=True)
    lane_row = lax.broadcasted_iota(jnp.int32, (1, LANES), 1)
    table_ref[blocks + 6 : blocks + 7, :] = jnp.where(
        lane_row == 0, ends[0], jnp.where(lane_row == 1, ends[1], every)
    ).astype(jnp.int32)


def sum_groups(half, blocks, terms, table_ref, bucket, acc, store):
    stride = terms + TILE
    acc[...] = jnp.zeros_like(acc)
    lane = lax.broadcasted_iota(jnp.int32, (LANES, LANES), 1)
    row_lane = lax.broadcasted_iota(jnp.int32, (1, CHUNK), 1)
    fold = LANES // stride

    def add_chunk(chunk):
        start = pl.multiple_of(table_ref[blocks + 3 * half, chunk] * TILE, TILE)
        left = table_ref[blocks + 3 * half + 1, chunk]
        group = table_ref[blocks + 3 * half + 2, chunk]
        part = bucket[pl.ds(start, CHUNK), :]
        codes = jnp.zeros((LANES, LANES), jnp.float32)
        spots = [(run % fold) * stride + terms + 2 * (run // fold) for run in range(CHUNK // LANES)]
        for run, spot in enumerate(spots):
            held = part[run * LANES : (run + 1) * LANES, 0:LANES].astype(jnp.float32)
            codes = jnp.where((lane == spot) | (lane == spot + 1), held, codes)
        codes = codes.T
        slot = jnp.concatenate(
            [codes[spot : spot + 1, :] * float(CODE) + codes[spot + 1 : spot + 2, :] for spot in spots],
            axis=1,
        ).astype(jnp.int32)
        slot = jnp.where(row_lane < left, slot, -1)
        incidence = (
            lax.broadcasted_iota(jnp.int32, (acc.shape[1], CHUNK), 0) == slot
        ).astype(jnp.bfloat16)
        acc[group] += jnp.dot(incidence, part, preferred_element_type=jnp.float32)

    def add_some(index, carry):
        for each in range(TOGETHER):
            add_chunk(index * TOGETHER + each)
        return carry

    number = table_ref[blocks + 6, half]
    lax.fori_loop(0, (number + TOGETHER - 1) // TOGETHER, add_some, 0)
    width = acc.shape[1]

    def finish(group, carry):
        result = acc[group].astype(store.dtype).T
        for index in range(MEMBERS):
            store[
                index // HALVES, group, :, (index % HALVES) * width : (index % HALVES + 1) * width
            ] = result[index * stride : index * stride + terms, :]
        return carry

    lax.fori_loop(0, acc.shape[0], finish, 0, unroll=2)


def sort_kernel(
    groups,
    trash_tile,
    size_ref,
    cols_ref,
    rho_ref,
    var_ref,
    signs_ref,
    low_ref,
    high_ref,
    genotype_ref,
    send_ref,
    bucket,
    plan_ref,
    rows_all,
    line_ref,
    member_ref,
    place_ref,
    table_ref,
    hot,
    cum,
    acc,
    arrived,
):
    prepare(
        groups,
        trash_tile,
        size_ref,
        cols_ref,
        rho_ref,
        var_ref,
        signs_ref,
        low_ref,
        high_ref,
        genotype_ref,
        rows_all,
        line_ref,
        member_ref,
        place_ref,
        plan_ref,
        hot,
        cum,
    )
    copy = pltpu.make_async_copy(plan_ref, table_ref, arrived)
    copy.start()
    copy.wait()
    rows, probes, cols = rows_all.shape[0] - 2, rows_all.shape[1], rows_all.shape[2]
    parts = cols // LANES
    pair = BLOCK // parts
    terms = 3 * probes
    stride = terms + TILE
    blocks = rows // pair
    staged_tiles = BLOCK * LANES // TILE + groups
    staged = staged_tiles * TILE
    col_pos = lax.broadcasted_iota(jnp.int32, (probes, cols), 1)

    def sort_block(block, carry):
        first = block * pair
        values, slopes = [], []
        for row in range(pair + 2):
            cells = rows_all[first + row]
            beside = jnp.where(col_pos == 0, 0.0, pltpu.roll(cells, 1, 1)) + jnp.where(
                col_pos == cols - 1, 0.0, pltpu.roll(cells, cols - 1, 1)
            )
            values.append(line_ref[0:1, :] * cells + line_ref[2:3, :] * beside)
            slopes.append(line_ref[1:2, :] * cells + line_ref[3:4, :] * beside)

        def segment(ref, row):
            at = first * parts + row * parts
            return jnp.concatenate(
                [ref[pl.ds(at + part, 1), :] for part in range(parts)], axis=1
            )

        blocks_of = []
        for row in range(pair):
            pos = size_ref[1] + first + row
            edge = (pos == 0) | (pos == size_ref[0] - 1)
            row_diag = jnp.where(edge, line_ref[6:7, :], line_ref[7:8, :])
            row_slope_diag = jnp.where(edge, line_ref[8:9, :], line_ref[9:10, :])
            scale = jnp.where(pos < size_ref[0], line_ref[10:11, :], 0.0)
            row_off, row_slope_off = line_ref[4:5, :], line_ref[5:6, :]
            value_beside = values[row] + values[row + 2]
            slope_beside = slopes[row] + slopes[row + 2]
            three = jnp.concatenate(
                [
                    (row_diag * values[row + 1] + row_off * value_beside) * scale,
                    (row_slope_diag * values[row + 1] + row_slope_off * value_beside) * scale,
                    (row_diag * slopes[row + 1] + row_off * slope_beside) * scale,
                ],
                axis=0,
            )
            member = segment(member_ref, row)
            slot = jnp.bitwise_and(segment(genotype_ref, row), G_DEV // HALVES - 1)
            code_row = lax.broadcasted_iota(jnp.int32, (TILE, cols), 0)
            code = jnp.where(
                jnp.bitwise_and(code_row, 1) == 0, lax.div(slot, CODE), lax.rem(slot, CODE)
            ).astype(jnp.float32)
            masked = []
            for index in range(MEMBERS):
                masked.append(jnp.where(member == index, three, 0.0))
                masked.append(code)
            blocks_of.append(jnp.concatenate(masked, axis=0).astype(jnp.bfloat16))
        payload = jnp.concatenate(blocks_of, axis=1)
        place = jnp.concatenate([segment(place_ref, row) for row in range(pair)], axis=1)
        chosen = (
            lax.broadcasted_iota(jnp.int32, (staged, BLOCK * LANES), 0) == place
        ).astype(jnp.bfloat16)
        ordered = lax.dot_general(
            chosen, payload, (((1,), (1,)), ((), ())), preferred_element_type=jnp.float32
        ).astype(jnp.bfloat16)
        for tile in range(staged_tiles):
            goal = pl.multiple_of(table_ref[block, tile] * TILE, TILE)
            bucket[pl.ds(goal, TILE), :] = ordered[tile * TILE : (tile + 1) * TILE, :]
        return carry

    lax.fori_loop(0, blocks, sort_block, 0, unroll=UNROLL)
    end = table_ref[blocks + 6, 2]
    clear = jnp.zeros((TILE, bucket.shape[1]), jnp.bfloat16)
    for tile in range(CHUNK // TILE):
        bucket[pl.ds(pl.multiple_of((end + tile) * TILE, TILE), TILE), :] = clear
    sum_groups(0, blocks, terms, table_ref, bucket, acc, send_ref)


def keep_kernel(blocks, table_ref, bucket, keep_ref, acc):
    sum_groups(1, blocks, keep_ref.shape[2], table_ref, bucket, acc, keep_ref)


def exchange(block, axis, bit):
    count = lax.axis_size(axis)
    return lax.ppermute(block, axis, [(i, i ^ bit) for i in range(count)])


def halve(total, names, name):
    at = names.index(name)
    mine = lax.index_in_dim(total, 0, at, keepdims=False)
    other = lax.index_in_dim(total, 1, at, keepdims=False).astype(jnp.bfloat16)
    return mine + exchange(other, *name).astype(jnp.float32), names[:at] + names[at + 1 :]


def body(probe_signs, trial_rows, trial_cols, ar_rho, res_var, plot_owner, plot_slot):
    probes, rows, cols = probe_signs.shape[0], probe_signs.shape[3], probe_signs.shape[4]
    trials, bands = lax.axis_size("trial"), lax.axis_size("geno")
    devices = trials * bands
    terms = 3 * probes
    stride = terms + TILE
    plots = rows * cols
    segments = plots // LANES
    parts = cols // LANES
    blocks = segments // BLOCK
    groups = devices // OWNERS
    band = lax.axis_index("geno")
    here = lax.axis_index("trial") * bands + band
    size = jnp.stack(
        [
            trial_rows[0],
            band * rows,
            jnp.int32(rows),
            jnp.int32(groups // 2),
        ]
    ).astype(jnp.int32)
    signs = probe_signs.reshape(probes, segments, LANES)
    vmem = pl.BlockSpec(memory_space=pltpu.VMEM)
    smem = pl.BlockSpec(memory_space=pltpu.SMEM)

    up = [(i, i + 1) for i in range(bands - 1)]
    low = lax.ppermute(signs[:, -parts:, :], "geno", up)
    high = lax.ppermute(signs[:, :parts, :], "geno", [(j, i) for i, j in up])

    genotype = (
        jnp.bitwise_xor(plot_owner.reshape(segments, LANES), here) * G_DEV
        + plot_slot.reshape(segments, LANES)
    )
    assert BLOCK * LANES // TILE + groups <= LANES and blocks < LANES
    assert plots // CHUNK + groups // 2 + TOGETHER <= LANES
    tiles = blocks * (BLOCK * LANES // TILE + groups)
    trash_tile = tiles + CHUNK // TILE
    bucket_shape = ((trash_tile + 1) * TILE, MEMBERS * stride)
    half = groups // 2
    acc_shape = (half, G_DEV // HALVES, MEMBERS * stride)
    out_shape = (OWNERS, half, terms, G_DEV)
    mib = 1024 * 1024
    bucket_bytes, acc_bytes = 2 * math.prod(bucket_shape), 4 * math.prod(acc_shape)
    plan_shape = (blocks + 8, LANES)
    send, bucket, plan = pl.pallas_call(
        functools.partial(sort_kernel, groups, trash_tile),
        out_shape=[
            jax.ShapeDtypeStruct(out_shape, jnp.bfloat16),
            jax.ShapeDtypeStruct(bucket_shape, jnp.bfloat16),
            jax.ShapeDtypeStruct(plan_shape, jnp.int32),
        ],
        in_specs=[smem] * 4 + [vmem] * 4,
        out_specs=[vmem] * 3,
        scratch_shapes=[
            pltpu.VMEM((rows + 2, probes, cols), jnp.float32),
            pltpu.VMEM((16, cols), jnp.float32),
            pltpu.VMEM((segments, LANES), jnp.int32),
            pltpu.VMEM((segments, LANES), jnp.int32),
            pltpu.SMEM(plan_shape, jnp.int32),
            pltpu.VMEM((segments * groups, LANES), jnp.float32),
            pltpu.VMEM((segments * groups, LANES), jnp.float32),
            pltpu.VMEM(acc_shape, jnp.float32),
            pltpu.SemaphoreType.DMA,
        ],
        compiler_params=pltpu.CompilerParams(
            vmem_limit_bytes=bucket_bytes
            + acc_bytes
            + 2 * math.prod(out_shape)
            + 8 * segments * groups * LANES
            + 10 * mib
        ),
        name="sort_plots",
    )(
        size,
        trial_cols,
        ar_rho,
        res_var,
        (2 * signs - 1).astype(jnp.float32),
        low,
        high,
        genotype,
    )
    received = exchange(send, "geno", 1)
    keep = pl.pallas_call(
        functools.partial(keep_kernel, blocks),
        out_shape=jax.ShapeDtypeStruct(out_shape, jnp.float32),
        in_specs=[smem, vmem],
        out_specs=vmem,
        scratch_shapes=[pltpu.VMEM(acc_shape, jnp.float32)],
        compiler_params=pltpu.CompilerParams(
            vmem_limit_bytes=bucket_bytes + acc_bytes + 4 * math.prod(out_shape) + 6 * mib
        ),
        cost_estimate=pl.CostEstimate(
            flops=2 * plots * MEMBERS * stride * G_DEV // HALVES, bytes_accessed=bucket_bytes, transcendentals=0
        ),
        name="sum_kept",
    )(plan, bucket)
    geno_bits, trial_bits = bands.bit_length() - 1, trials.bit_length() - 1
    names = [("geno", 2)]
    names += [("trial", 1 << i) for i in reversed(range(trial_bits))]
    names += [("geno", 1 << i) for i in reversed(range(2, geno_bits))]
    dims = [("geno", 2)] + [("trial", 1 << i) for i in range(trial_bits)]
    dims += [("geno", 1 << i) for i in range(2, geno_bits)]
    shape = [2] * len(dims)
    keep = keep.reshape(shape + [3, probes, G_DEV])
    received = received.reshape(shape + [3, probes, G_DEV])
    lead = min(3, len(dims))
    totals, lefts = [], []
    for part in range(3):
        total = keep[..., part, :, :] + received[..., part, :, :].astype(jnp.float32)
        left = list(names)
        for step in range(lead):
            total, left = halve(total, left, dims[(part + step) % lead])
        totals.append(total)
    total = jnp.stack(totals, -3)
    for name in dims[lead:]:
        total, left = halve(total, left, name)
    return total


def solution(mesh):
    return jax.shard_map(
        body,
        mesh=mesh,
        in_specs=(
            P(None, ("trial", "geno"), None, None, None),
            P("trial"),
            P("trial"),
            P("trial", None),
            P("trial"),
            P(("trial", "geno"), None, None, None, None),
            P(("trial", "geno"), None, None, None),
        ),
        out_specs=P(None, None, ("trial", "geno")),
        check_vma=False,
    )
```

```python
import functools
import math

import jax
import jax.numpy as jnp
from jax import lax
from jax.experimental import pallas as pl
from jax.experimental.pallas import tpu as pltpu
from jax.sharding import PartitionSpec as P

G_DEV = 1024
TILE = 16
CHUNK = 512
BLOCK = 4
LANES = 128
HALVES = 2
OWNERS = 2
MEMBERS = HALVES * OWNERS
UNROLL = 11
TOGETHER = 8
CODE = 32


def round_up(value, step):
    return -(-value // step) * step


def bits_to_field(bits, row_in, col_in):
    return jnp.where(row_in & col_in, 2.0 * bits.astype(jnp.float32) - 1.0, 0.0)


def place_of(params_ref, rows):
    band = lax.axis_index("geno")
    trial_rows = params_ref[0, 0].astype(jnp.int32)
    return trial_rows, band * rows, lax.axis_index("trial") * lax.axis_size("geno") + band


def prepare(
    signs_load,
    groups,
    trash_tile,
    params_ref,
    signs_ref,
    low_ref,
    high_ref,
    owner_ref,
    slot_ref,
    field_ref,
    line_ref,
    member_ref,
    place_ref,
    table_ref,
    hot,
    cum,
):
    rows, probes, cols = field_ref.shape[0] - 2, field_ref.shape[1], field_ref.shape[2]
    parts = cols // LANES
    segments = rows * parts
    blocks = segments // BLOCK
    trial_rows, first_row, device = place_of(params_ref, rows)
    trial_cols = params_ref[0, 1].astype(jnp.int32)
    pos = lax.broadcasted_iota(jnp.int32, (1, cols), 1)
    flat = jnp.zeros((1, cols), jnp.float32)
    rho = flat + params_ref[0, 3]
    inverse = 1.0 / (1.0 - rho * rho)
    inside = 1.0 + rho * rho
    edge = (pos == 0) | (pos == trial_cols - 1)
    line_ref[0:1, :] = jnp.where(edge, inverse, inverse * inside)
    line_ref[1:2, :] = jnp.where(
        edge, 2.0 * rho * inverse * inverse, 4.0 * rho * inverse * inverse
    )
    line_ref[2:3, :] = -inverse * rho
    line_ref[3:4, :] = -inside * inverse * inverse
    rho = flat + params_ref[0, 2]
    inverse = 1.0 / (1.0 - rho * rho)
    inside = 1.0 + rho * rho
    line_ref[4:5, :] = -inverse * rho
    line_ref[5:6, :] = -inside * inverse * inverse
    line_ref[6:7, :] = inverse
    line_ref[7:8, :] = inverse * inside
    line_ref[8:9, :] = 2.0 * rho * inverse * inverse
    line_ref[9:10, :] = 4.0 * rho * inverse * inverse
    line_ref[10:11, :] = jnp.where(pos < trial_cols, 1.0 / (flat + params_ref[0, 4]), 0.0)
    owner = jnp.bitwise_xor(owner_ref[...], device)
    rest = lax.shift_right_logical(owner, 1)
    group_of = lax.shift_right_logical(rest, 1) + jnp.where(
        jnp.bitwise_and(owner, 1) == 1, 0, groups // 2
    )
    slot = slot_ref[...]
    member_ref[...] = jnp.bitwise_and(rest, 1) * HALVES + jnp.where(
        slot >= G_DEV // HALVES, 1, 0
    )
    group_id = lax.broadcasted_iota(jnp.int32, (groups, LANES), 0)
    for seg in range(segments):
        hot[seg * groups : (seg + 1) * groups, :] = (
            group_of[seg : seg + 1, :] == group_id
        ).astype(jnp.float32)
    square = (LANES, LANES)
    upper = lax.broadcasted_iota(jnp.int32, square, 0) <= lax.broadcasted_iota(jnp.int32, square, 1)
    before = lax.broadcasted_iota(jnp.int32, square, 0) < lax.broadcasted_iota(jnp.int32, square, 1)
    cum[...] = jnp.dot(
        hot[...].astype(jnp.bfloat16),
        upper.astype(jnp.bfloat16),
        preferred_element_type=jnp.float32,
    )
    lane = lax.broadcasted_iota(jnp.int32, (groups, LANES), 1)
    counts = jnp.zeros((groups, LANES), jnp.float32)
    for block in range(blocks):
        total = jnp.zeros((groups, 1), jnp.float32)
        for seg in range(block * BLOCK, (block + 1) * BLOCK):
            total = total + cum[seg * groups : (seg + 1) * groups, LANES - 1 : LANES]
        counts = jnp.where(lane == block, total, counts)
    tiles = jnp.floor((counts + (TILE - 1.0)) * (1.0 / TILE))
    above = (
        lax.broadcasted_iota(jnp.int32, (groups, groups), 1)
        < lax.broadcasted_iota(jnp.int32, (groups, groups), 0)
    ).astype(jnp.bfloat16)
    tiles_bf = tiles.astype(jnp.bfloat16)
    earlier = jnp.dot(tiles_bf, before.astype(jnp.bfloat16), preferred_element_type=jnp.float32)
    starts = jnp.dot(above, tiles_bf, preferred_element_type=jnp.float32)
    base = jnp.sum(starts, axis=1, keepdims=True)
    lane_f = lane.astype(jnp.float32)
    for block in range(blocks):
        start = starts[:, block : block + 1]
        number = tiles[:, block : block + 1]
        offset = start * float(TILE) - 1.0
        for seg in range(block * BLOCK, (block + 1) * BLOCK):
            here = slice(seg * groups, (seg + 1) * groups)
            place_ref[seg : seg + 1, :] = jnp.sum(
                hot[here, :] * (cum[here, :] + offset), axis=0, keepdims=True
            ).astype(jnp.int32)
            offset = offset + cum[here, LANES - 1 : LANES]
        held = (lane_f >= start) & (lane_f < start + number)
        goal = base + earlier[:, block : block + 1] + lane_f - start
        chosen = jnp.sum(jnp.where(held, goal + 1.0, 0.0), axis=0, keepdims=True)
        table_ref[block : block + 1, :] = jnp.where(
            chosen > 0.0, chosen - 1.0, float(trash_tile)
        ).astype(jnp.int32)
    total = earlier[:, blocks : blocks + 1]
    step = float(CHUNK // TILE)
    chunks = jnp.floor((total + (step - 1.0)) * (1.0 / step))
    group_row = lax.broadcasted_iota(jnp.int32, (groups, LANES), 0)
    ends = []
    for half in range(2):
        mine = (group_row >= half * (groups // 2)) & (group_row < (half + 1) * (groups // 2))
        own = jnp.where(mine, chunks, 0.0)
        first = jnp.dot(above, own.astype(jnp.bfloat16), preferred_element_type=jnp.float32)
        held = mine & (lane_f >= first) & (lane_f < first + own)
        index = lane_f - first
        fields = (
            base + step * index,
            (total - step * index) * float(TILE),
            (group_row - half * (groups // 2)).astype(jnp.float32),
        )
        for row, value in enumerate(fields):
            at = blocks + 3 * half + row
            table_ref[at : at + 1, :] = jnp.sum(
                jnp.where(held, value, 0.0), axis=0, keepdims=True
            ).astype(jnp.int32)
        ends.append(jnp.sum(own, axis=0, keepdims=True))
    every = jnp.sum(total + jnp.zeros((groups, LANES), jnp.float32), axis=0, keepdims=True)
    lane_row = lax.broadcasted_iota(jnp.int32, (1, LANES), 1)
    table_ref[blocks + 6 : blocks + 7, :] = jnp.where(
        lane_row == 0, ends[0], jnp.where(lane_row == 1, ends[1], every)
    ).astype(jnp.int32)
    signs_load.wait()
    for part in range(parts):
        col_in = (
            lax.broadcasted_iota(jnp.int32, (probes, LANES), 1) + part * LANES < trial_cols
        )
        here = slice(part * LANES, (part + 1) * LANES)
        for row in range(rows):
            field_ref[row + 1, :, here] = bits_to_field(
                signs_ref[:, row * parts + part, :], first_row + row < trial_rows, col_in
            )
        field_ref[0, :, here] = bits_to_field(
            low_ref[:, part, :], (first_row > 0) & (first_row <= trial_rows), col_in
        )
        field_ref[rows + 1, :, here] = bits_to_field(
            high_ref[:, part, :], first_row + rows < trial_rows, col_in
        )


def sum_groups(half, blocks, terms, table_ref, bucket, acc, store):
    stride = terms + TILE
    acc[...] = jnp.zeros_like(acc)
    lane = lax.broadcasted_iota(jnp.int32, (LANES, LANES), 1)
    row_lane = lax.broadcasted_iota(jnp.int32, (1, CHUNK), 1)
    fold = LANES // stride

    def add_chunk(chunk):
        start = pl.multiple_of(table_ref[blocks + 3 * half, chunk] * TILE, TILE)
        left = table_ref[blocks + 3 * half + 1, chunk]
        group = table_ref[blocks + 3 * half + 2, chunk]
        part = bucket[pl.ds(start, CHUNK), :]
        codes = jnp.zeros((LANES, LANES), jnp.float32)
        spots = [(run % fold) * stride + terms + 2 * (run // fold) for run in range(CHUNK // LANES)]
        for run, spot in enumerate(spots):
            held = part[run * LANES : (run + 1) * LANES, 0:LANES].astype(jnp.float32)
            codes = jnp.where((lane == spot) | (lane == spot + 1), held, codes)
        codes = codes.T
        slot = jnp.concatenate(
            [codes[spot : spot + 1, :] * float(CODE) + codes[spot + 1 : spot + 2, :] for spot in spots],
            axis=1,
        ).astype(jnp.int32)
        slot = jnp.where(row_lane < left, slot, -1)
        incidence = (
            lax.broadcasted_iota(jnp.int32, (acc.shape[1], CHUNK), 0) == slot
        ).astype(jnp.bfloat16)
        acc[group] += jnp.dot(incidence, part, preferred_element_type=jnp.float32)

    def add_some(index, carry):
        for each in range(TOGETHER):
            add_chunk(index * TOGETHER + each)
        return carry

    number = table_ref[blocks + 6, half]
    lax.fori_loop(0, (number + TOGETHER - 1) // TOGETHER, add_some, 0)
    width = acc.shape[1]

    def finish(group, carry):
        result = acc[group].astype(store.dtype).T
        for index in range(MEMBERS):
            store[
                index // HALVES, group, :, (index % HALVES) * width : (index % HALVES + 1) * width
            ] = result[index * stride : index * stride + terms, :]
        return carry

    lax.fori_loop(0, acc.shape[0], finish, 0, unroll=2)


def sort_kernel(
    groups,
    trash_tile,
    params_vmem,
    signs_hbm,
    owner_hbm,
    slot_hbm,
    low_ref,
    high_ref,
    send_ref,
    bucket,
    plan_ref,
    params_ref,
    signs_ref,
    owner_ref,
    slot_ref,
    rows_all,
    line_ref,
    member_ref,
    place_ref,
    table_ref,
    hot,
    cum,
    acc,
    loaded,
    arrived,
):
    loads = [
        pltpu.make_async_copy(source, target, loaded.at[index])
        for index, (source, target) in enumerate(
            (
                (signs_hbm, signs_ref),
                (owner_hbm, owner_ref),
                (slot_hbm, slot_ref),
                (params_vmem, params_ref),
            )
        )
    ]
    for load in loads:
        load.start()
    for load in loads[1:]:
        load.wait()
    prepare(
        loads[0],
        groups,
        trash_tile,
        params_ref,
        signs_ref,
        low_ref,
        high_ref,
        owner_ref,
    slot_ref,
        rows_all,
        line_ref,
        member_ref,
        place_ref,
        plan_ref,
        hot,
        cum,
    )
    copy = pltpu.make_async_copy(plan_ref, table_ref, arrived)
    copy.start()
    copy.wait()
    rows, probes, cols = rows_all.shape[0] - 2, rows_all.shape[1], rows_all.shape[2]
    parts = cols // LANES
    pair = BLOCK // parts
    terms = 3 * probes
    stride = terms + TILE
    blocks = rows // pair
    staged_tiles = BLOCK * LANES // TILE + groups
    staged = staged_tiles * TILE
    trial_rows, first_row, _ = place_of(params_ref, rows)
    col_pos = lax.broadcasted_iota(jnp.int32, (probes, cols), 1)

    def sort_block(block, carry):
        first = block * pair
        values, slopes = [], []
        for row in range(pair + 2):
            cells = rows_all[first + row]
            beside = jnp.where(col_pos == 0, 0.0, pltpu.roll(cells, 1, 1)) + jnp.where(
                col_pos == cols - 1, 0.0, pltpu.roll(cells, cols - 1, 1)
            )
            values.append(line_ref[0:1, :] * cells + line_ref[2:3, :] * beside)
            slopes.append(line_ref[1:2, :] * cells + line_ref[3:4, :] * beside)

        def segment(ref, row):
            at = first * parts + row * parts
            return jnp.concatenate(
                [ref[pl.ds(at + part, 1), :] for part in range(parts)], axis=1
            )

        blocks_of = []
        for row in range(pair):
            pos = first_row + first + row
            edge = (pos == 0) | (pos == trial_rows - 1)
            row_diag = jnp.where(edge, line_ref[6:7, :], line_ref[7:8, :])
            row_slope_diag = jnp.where(edge, line_ref[8:9, :], line_ref[9:10, :])
            scale = jnp.where(pos < trial_rows, line_ref[10:11, :], 0.0)
            row_off, row_slope_off = line_ref[4:5, :], line_ref[5:6, :]
            value_beside = values[row] + values[row + 2]
            slope_beside = slopes[row] + slopes[row + 2]
            three = jnp.concatenate(
                [
                    (row_diag * values[row + 1] + row_off * value_beside) * scale,
                    (row_slope_diag * values[row + 1] + row_slope_off * value_beside) * scale,
                    (row_diag * slopes[row + 1] + row_off * slope_beside) * scale,
                ],
                axis=0,
            )
            member = segment(member_ref, row)
            slot = jnp.bitwise_and(segment(slot_ref, row), G_DEV // HALVES - 1)
            code_row = lax.broadcasted_iota(jnp.int32, (TILE, cols), 0)
            code = jnp.where(
                jnp.bitwise_and(code_row, 1) == 0, lax.div(slot, CODE), lax.rem(slot, CODE)
            ).astype(jnp.float32)
            masked = []
            for index in range(MEMBERS):
                masked.append(jnp.where(member == index, three, 0.0))
                masked.append(code)
            blocks_of.append(jnp.concatenate(masked, axis=0).astype(jnp.bfloat16))
        payload = jnp.concatenate(blocks_of, axis=1)
        place = jnp.concatenate([segment(place_ref, row) for row in range(pair)], axis=1)
        chosen = (
            lax.broadcasted_iota(jnp.int32, (staged, BLOCK * LANES), 0) == place
        ).astype(jnp.bfloat16)
        ordered = lax.dot_general(
            chosen, payload, (((1,), (1,)), ((), ())), preferred_element_type=jnp.float32
        ).astype(jnp.bfloat16)
        for tile in range(staged_tiles):
            goal = pl.multiple_of(table_ref[block, tile] * TILE, TILE)
            bucket[pl.ds(goal, TILE), :] = ordered[tile * TILE : (tile + 1) * TILE, :]
        return carry

    lax.fori_loop(0, blocks, sort_block, 0, unroll=UNROLL)
    end = table_ref[blocks + 6, 2]
    clear = jnp.zeros((TILE, bucket.shape[1]), jnp.bfloat16)
    for tile in range(CHUNK // TILE):
        bucket[pl.ds(pl.multiple_of((end + tile) * TILE, TILE), TILE), :] = clear
    sum_groups(0, blocks, terms, table_ref, bucket, acc, send_ref)


def keep_kernel(blocks, table_ref, bucket, keep_ref, acc):
    sum_groups(1, blocks, keep_ref.shape[2], table_ref, bucket, acc, keep_ref)


def exchange(block, axis, bit):
    count = lax.axis_size(axis)
    return lax.ppermute(block, axis, [(i, i ^ bit) for i in range(count)])


def halve(total, names, name):
    at = names.index(name)
    mine = lax.index_in_dim(total, 0, at, keepdims=False)
    other = lax.index_in_dim(total, 1, at, keepdims=False).astype(jnp.bfloat16)
    return mine + exchange(other, *name).astype(jnp.float32), names[:at] + names[at + 1 :]


def body(probe_signs, trial_rows, trial_cols, ar_rho, res_var, plot_owner, plot_slot):
    probes, rows, cols = probe_signs.shape[0], probe_signs.shape[3], probe_signs.shape[4]
    trials, bands = lax.axis_size("trial"), lax.axis_size("geno")
    devices = trials * bands
    terms = 3 * probes
    stride = terms + TILE
    plots = rows * cols
    segments = plots // LANES
    parts = cols // LANES
    blocks = segments // BLOCK
    groups = devices // OWNERS
    signs = probe_signs.reshape(probes, segments, LANES)
    vmem = pl.BlockSpec(memory_space=pltpu.VMEM)
    smem = pl.BlockSpec(memory_space=pltpu.SMEM)

    up = [(i, i + 1) for i in range(bands - 1)]
    low = lax.ppermute(signs[:, -parts:, :], "geno", up)
    high = lax.ppermute(signs[:, :parts, :], "geno", [(j, i) for i, j in up])

    assert BLOCK * LANES // TILE + groups <= LANES and blocks < LANES
    assert plots // CHUNK + groups // 2 + TOGETHER <= LANES
    tiles = blocks * (BLOCK * LANES // TILE + groups)
    trash_tile = tiles + CHUNK // TILE
    bucket_shape = ((trash_tile + 1) * TILE, MEMBERS * stride)
    half = groups // 2
    acc_shape = (half, G_DEV // HALVES, MEMBERS * stride)
    out_shape = (OWNERS, half, terms, G_DEV)
    mib = 1024 * 1024
    bucket_bytes, acc_bytes = 2 * math.prod(bucket_shape), 4 * math.prod(acc_shape)
    plan_shape = (blocks + 8, LANES)
    params = jnp.concatenate(
        [trial_rows.astype(jnp.float32), trial_cols.astype(jnp.float32), ar_rho[0], res_var]
    )
    params = jnp.pad(params[None], ((0, 7), (0, LANES - params.shape[0])))
    send, bucket, plan = pl.pallas_call(
        functools.partial(sort_kernel, groups, trash_tile),
        out_shape=[
            jax.ShapeDtypeStruct(out_shape, jnp.bfloat16),
            jax.ShapeDtypeStruct(bucket_shape, jnp.bfloat16),
            jax.ShapeDtypeStruct(plan_shape, jnp.int32),
        ],
        in_specs=[vmem] + [pl.BlockSpec(memory_space=pltpu.HBM)] * 3 + [vmem] * 2,
        out_specs=[vmem] * 3,
        scratch_shapes=[
            pltpu.SMEM((8, LANES), jnp.float32),
            pltpu.VMEM((probes, segments, LANES), jnp.int32),
            pltpu.VMEM((segments, LANES), jnp.int32),
            pltpu.VMEM((segments, LANES), jnp.int32),
            pltpu.VMEM((rows + 2, probes, cols), jnp.float32),
            pltpu.VMEM((16, cols), jnp.float32),
            pltpu.VMEM((segments, LANES), jnp.int32),
            pltpu.VMEM((segments, LANES), jnp.int32),
            pltpu.SMEM(plan_shape, jnp.int32),
            pltpu.VMEM((segments * groups, LANES), jnp.float32),
            pltpu.VMEM((segments * groups, LANES), jnp.float32),
            pltpu.VMEM(acc_shape, jnp.float32),
            pltpu.SemaphoreType.DMA((4,)),
            pltpu.SemaphoreType.DMA,
        ],
        compiler_params=pltpu.CompilerParams(
            vmem_limit_bytes=bucket_bytes
            + acc_bytes
            + 2 * math.prod(out_shape)
            + 8 * segments * groups * LANES
            + 10 * mib
        ),
        name="sort_plots",
    )(
        params,
        *[
            pltpu.with_memory_space_constraint(operand, pltpu.HBM)
            for operand in (
                signs,
                plot_owner.reshape(segments, LANES),
                plot_slot.reshape(segments, LANES),
            )
        ],
        low,
        high,
    )
    received = exchange(send, "geno", 1)
    keep = pl.pallas_call(
        functools.partial(keep_kernel, blocks),
        out_shape=jax.ShapeDtypeStruct(out_shape, jnp.float32),
        in_specs=[smem, vmem],
        out_specs=vmem,
        scratch_shapes=[pltpu.VMEM(acc_shape, jnp.float32)],
        compiler_params=pltpu.CompilerParams(
            vmem_limit_bytes=bucket_bytes + acc_bytes + 4 * math.prod(out_shape) + 6 * mib
        ),
        cost_estimate=pl.CostEstimate(
            flops=2 * plots * MEMBERS * stride * G_DEV // HALVES, bytes_accessed=bucket_bytes, transcendentals=0
        ),
        name="sum_kept",
    )(plan, bucket)
    geno_bits, trial_bits = bands.bit_length() - 1, trials.bit_length() - 1
    names = [("geno", 2)]
    names += [("trial", 1 << i) for i in reversed(range(trial_bits))]
    names += [("geno", 1 << i) for i in reversed(range(2, geno_bits))]
    dims = [("geno", 2)] + [("trial", 1 << i) for i in range(trial_bits)]
    dims += [("geno", 1 << i) for i in range(2, geno_bits)]
    shape = [2] * len(dims)
    keep = keep.reshape(shape + [3, probes, G_DEV])
    received = received.reshape(shape + [3, probes, G_DEV])
    lead = min(3, len(dims))
    totals, lefts = [], []
    for part in range(3):
        total = keep[..., part, :, :] + received[..., part, :, :].astype(jnp.float32)
        left = list(names)
        for step in range(lead):
            total, left = halve(total, left, dims[(part + step) % lead])
        totals.append(total)
    total = jnp.stack(totals, -3)
    for name in dims[lead:]:
        total, left = halve(total, left, name)
    return total


def solution(mesh):
    return jax.shard_map(
        body,
        mesh=mesh,
        in_specs=(
            P(None, ("trial", "geno"), None, None, None),
            P("trial"),
            P("trial"),
            P("trial", None),
            P("trial"),
            P(("trial", "geno"), None, None, None, None),
            P(("trial", "geno"), None, None, None),
        ),
        out_specs=P(None, None, ("trial", "geno")),
        check_vma=False,
    )
```

```python
import functools
import math

import jax
import jax.numpy as jnp
from jax import lax
from jax.experimental import pallas as pl
from jax.experimental.pallas import tpu as pltpu
from jax.sharding import PartitionSpec as P

G_DEV = 1024
TILE = 16
CHUNK = 512
BLOCK = 4
LANES = 128
HALVES = 2
OWNERS = 2
MEMBERS = HALVES * OWNERS
UNROLL = 22
TOGETHER = 8
REST = 2
CODE = 32


def round_up(value, step):
    return -(-value // step) * step


def bits_to_field(bits, row_in, col_in):
    return jnp.where(row_in & col_in, 2.0 * bits.astype(jnp.float32) - 1.0, 0.0)


def place_of(size_ref, rows):
    band = lax.axis_index("geno")
    trial_rows = size_ref[0]
    return trial_rows, band * rows, lax.axis_index("trial") * lax.axis_size("geno") + band


def prepare(
    loads,
    groups,
    trash_tile,
    size_ref,
    cols_ref,
    var_ref,
    rho_ref,
    signs_ref,
    near_ref,
    far_ref,
    owner_ref,
    slot_ref,
    field_ref,
    line_ref,
    member_ref,
    place_ref,
    table_ref,
    table_smem,
    hot,
    cum,
    arrived,
):
    rows, probes, cols = field_ref.shape[0] - 2, field_ref.shape[1], field_ref.shape[2]
    parts = cols // LANES
    segments = rows * parts
    blocks = segments // BLOCK
    trial_rows, first_row, device = place_of(size_ref, rows)
    trial_cols = cols_ref[0]
    odd = lax.rem(lax.axis_index("geno"), 2) == 1
    loads[3].wait()
    pos = lax.broadcasted_iota(jnp.int32, (1, cols), 1)
    flat = jnp.zeros((1, cols), jnp.float32)
    rho = flat + rho_ref[0, 1]
    inverse = 1.0 / (1.0 - rho * rho)
    inside = 1.0 + rho * rho
    edge = (pos == 0) | (pos == trial_cols - 1)
    line_ref[0:1, :] = jnp.where(edge, inverse, inverse * inside)
    line_ref[1:2, :] = jnp.where(
        edge, 2.0 * rho * inverse * inverse, 4.0 * rho * inverse * inverse
    )
    line_ref[2:3, :] = -inverse * rho
    line_ref[3:4, :] = -inside * inverse * inverse
    rho = flat + rho_ref[0, 0]
    inverse = 1.0 / (1.0 - rho * rho)
    inside = 1.0 + rho * rho
    line_ref[4:5, :] = -inverse * rho
    line_ref[5:6, :] = -inside * inverse * inverse
    line_ref[6:7, :] = inverse
    line_ref[7:8, :] = inverse * inside
    line_ref[8:9, :] = 2.0 * rho * inverse * inverse
    line_ref[9:10, :] = 4.0 * rho * inverse * inverse
    line_ref[10:11, :] = jnp.where(pos < trial_cols, 1.0 / (flat + var_ref[0]), 0.0)
    loads[1].wait()
    loads[2].wait()
    owner = jnp.bitwise_xor(owner_ref[...], device)
    rest = lax.shift_right_logical(owner, 1)
    group_of = lax.shift_right_logical(rest, 1) + jnp.where(
        jnp.bitwise_and(owner, 1) == 1, 0, groups // 2
    )
    slot = slot_ref[...]
    member_ref[...] = jnp.bitwise_and(rest, 1) * HALVES + jnp.where(
        slot >= G_DEV // HALVES, 1, 0
    )
    group_id = lax.broadcasted_iota(jnp.int32, (groups, LANES), 0)
    for seg in range(segments):
        hot[seg * groups : (seg + 1) * groups, :] = (
            group_of[seg : seg + 1, :] == group_id
        ).astype(jnp.float32)
    square = (LANES, LANES)
    upper = lax.broadcasted_iota(jnp.int32, square, 0) <= lax.broadcasted_iota(jnp.int32, square, 1)
    before = lax.broadcasted_iota(jnp.int32, square, 0) < lax.broadcasted_iota(jnp.int32, square, 1)
    cum[...] = jnp.dot(
        hot[...].astype(jnp.bfloat16),
        upper.astype(jnp.bfloat16),
        preferred_element_type=jnp.float32,
    )
    lane = lax.broadcasted_iota(jnp.int32, (groups, LANES), 1)
    counts = jnp.zeros((groups, LANES), jnp.float32)
    for block in range(blocks):
        total = jnp.zeros((groups, 1), jnp.float32)
        for seg in range(block * BLOCK, (block + 1) * BLOCK):
            total = total + cum[seg * groups : (seg + 1) * groups, LANES - 1 : LANES]
        counts = jnp.where(lane == block, total, counts)
    tiles = jnp.floor((counts + (TILE - 1.0)) * (1.0 / TILE))
    above = (
        lax.broadcasted_iota(jnp.int32, (groups, groups), 1)
        < lax.broadcasted_iota(jnp.int32, (groups, groups), 0)
    ).astype(jnp.bfloat16)
    tiles_bf = tiles.astype(jnp.bfloat16)
    earlier = jnp.dot(tiles_bf, before.astype(jnp.bfloat16), preferred_element_type=jnp.float32)
    starts = jnp.dot(above, tiles_bf, preferred_element_type=jnp.float32)
    base = jnp.sum(starts, axis=1, keepdims=True)
    lane_f = lane.astype(jnp.float32)
    for block in range(blocks):
        start = starts[:, block : block + 1]
        number = tiles[:, block : block + 1]
        offset = start * float(TILE) - 1.0
        for seg in range(block * BLOCK, (block + 1) * BLOCK):
            here = slice(seg * groups, (seg + 1) * groups)
            place_ref[seg : seg + 1, :] = jnp.sum(
                hot[here, :] * (cum[here, :] + offset), axis=0, keepdims=True
            ).astype(jnp.int32)
            offset = offset + cum[here, LANES - 1 : LANES]
        held = (lane_f >= start) & (lane_f < start + number)
        goal = base + earlier[:, block : block + 1] + lane_f - start
        chosen = jnp.sum(jnp.where(held, goal + 1.0, 0.0), axis=0, keepdims=True)
        table_ref[block : block + 1, :] = jnp.where(
            chosen > 0.0, chosen - 1.0, float(trash_tile)
        ).astype(jnp.int32)
    total = earlier[:, blocks : blocks + 1]
    step = float(CHUNK // TILE)
    chunks = jnp.floor((total + (step - 1.0)) * (1.0 / step))
    group_row = lax.broadcasted_iota(jnp.int32, (groups, LANES), 0)
    ends = []
    for half in range(2):
        mine = (group_row >= half * (groups // 2)) & (group_row < (half + 1) * (groups // 2))
        own = jnp.where(mine, chunks, 0.0)
        first = jnp.dot(above, own.astype(jnp.bfloat16), preferred_element_type=jnp.float32)
        held = mine & (lane_f >= first) & (lane_f < first + own)
        index = lane_f - first
        fields = (
            base + step * index,
            (total - step * index) * float(TILE),
            (group_row - half * (groups // 2)).astype(jnp.float32),
        )
        for row, value in enumerate(fields):
            at = blocks + 3 * half + row
            table_ref[at : at + 1, :] = jnp.sum(
                jnp.where(held, value, 0.0), axis=0, keepdims=True
            ).astype(jnp.int32)
        ends.append(jnp.sum(own, axis=0, keepdims=True))
    every = jnp.sum(total + jnp.zeros((groups, LANES), jnp.float32), axis=0, keepdims=True)
    lane_row = lax.broadcasted_iota(jnp.int32, (1, LANES), 1)
    table_ref[blocks + 6 : blocks + 7, :] = jnp.where(
        lane_row == 0, ends[0], jnp.where(lane_row == 1, ends[1], every)
    ).astype(jnp.int32)
    copy = pltpu.make_async_copy(table_ref, table_smem, arrived)
    copy.start()
    loads[0].wait()
    for part in range(parts):
        col_in = (
            lax.broadcasted_iota(jnp.int32, (probes, LANES), 1) + part * LANES < trial_cols
        )
        here = slice(part * LANES, (part + 1) * LANES)
        for row in range(rows):
            field_ref[row + 1, :, here] = bits_to_field(
                signs_ref[:, row * parts + part, :], first_row + row < trial_rows, col_in
            )
        low = jnp.where(odd, near_ref[:, parts + part, :], far_ref[:, parts + part, :])
        field_ref[0, :, here] = bits_to_field(
            low, (first_row > 0) & (first_row <= trial_rows), col_in
        )
        high = jnp.where(odd, far_ref[:, part, :], near_ref[:, part, :])
        field_ref[rows + 1, :, here] = bits_to_field(
            high, first_row + rows < trial_rows, col_in
        )
    copy.wait()


def sum_groups(half, blocks, terms, table_ref, bucket, acc, stores):
    stride = terms + TILE
    lane = lax.broadcasted_iota(jnp.int32, (LANES, LANES), 1)
    row_lane = lax.broadcasted_iota(jnp.int32, (1, CHUNK), 1)
    fold = LANES // stride

    def add_chunk(chunk):
        start = pl.multiple_of(table_ref[blocks + 3 * half, chunk] * TILE, TILE)
        left = table_ref[blocks + 3 * half + 1, chunk]
        group = table_ref[blocks + 3 * half + 2, chunk]
        part = bucket[pl.ds(start, CHUNK), :]
        codes = jnp.zeros((LANES, LANES), jnp.float32)
        spots = [(run % fold) * stride + terms + 2 * (run // fold) for run in range(CHUNK // LANES)]
        for run, spot in enumerate(spots):
            held = part[run * LANES : (run + 1) * LANES, 0:LANES].astype(jnp.float32)
            codes = jnp.where((lane == spot) | (lane == spot + 1), held, codes)
        codes = codes.T
        slot = jnp.concatenate(
            [codes[spot : spot + 1, :] * float(CODE) + codes[spot + 1 : spot + 2, :] for spot in spots],
            axis=1,
        ).astype(jnp.int32)
        slot = jnp.where(row_lane < left, slot, -1)
        incidence = (
            lax.broadcasted_iota(jnp.int32, (acc.shape[1], CHUNK), 0) == slot
        ).astype(jnp.bfloat16)
        acc[group] += jnp.dot(incidence, part, preferred_element_type=jnp.float32)

    def add_some(together, first, index, carry):
        for each in range(together):
            add_chunk(first + index * together + each)
        return carry

    number = table_ref[blocks + 6, half]
    most = lax.div(number, TOGETHER)
    lax.fori_loop(0, most, functools.partial(add_some, TOGETHER, 0), 0)
    rest = number - most * TOGETHER
    lax.fori_loop(
        0, lax.div(rest + REST - 1, REST), functools.partial(add_some, REST, most * TOGETHER), 0
    )
    width = acc.shape[1]

    def finish(group, carry):
        result = acc[group].astype(stores[0].dtype).T
        for index in range(MEMBERS):
            at = index * stride
            for store in stores:
                store[
                    index // HALVES, group, :, (index % HALVES) * width : (index % HALVES + 1) * width
                ] = result[at : at + store.shape[2], :]
                at += store.shape[2]
        return carry

    lax.fori_loop(0, acc.shape[0], finish, 0, unroll=2)


def sort_kernel(
    groups,
    trash_tile,
    size_ref,
    cols_ref,
    var_ref,
    rho_hbm,
    signs_hbm,
    owner_hbm,
    slot_hbm,
    near_ref,
    far_ref,
    send_ref,
    bucket,
    plan_ref,
    rho_ref,
    signs_ref,
    owner_ref,
    slot_ref,
    rows_all,
    line_ref,
    member_ref,
    place_ref,
    table_ref,
    hot,
    cum,
    acc,
    loaded,
    arrived,
):
    loads = [
        pltpu.make_async_copy(source, target, loaded.at[index])
        for index, (source, target) in enumerate(
            (
                (signs_hbm, signs_ref),
                (owner_hbm, owner_ref),
                (slot_hbm, slot_ref),
                (rho_hbm, rho_ref),
            )
        )
    ]
    for load in loads:
        load.start()
    acc[...] = jnp.zeros_like(acc)
    prepare(
        loads,
        groups,
        trash_tile,
        size_ref,
        cols_ref,
        var_ref,
        rho_ref,
        signs_ref,
        near_ref,
        far_ref,
        owner_ref,
    slot_ref,
        rows_all,
        line_ref,
        member_ref,
        place_ref,
        plan_ref,
        table_ref,
        hot,
        cum,
        arrived,
    )
    rows, probes, cols = rows_all.shape[0] - 2, rows_all.shape[1], rows_all.shape[2]
    parts = cols // LANES
    pair = BLOCK // parts
    terms = 3 * probes
    stride = terms + TILE
    blocks = rows // pair
    staged_tiles = BLOCK * LANES // TILE + groups
    staged = staged_tiles * TILE
    trial_rows, first_row, _ = place_of(size_ref, rows)
    col_pos = lax.broadcasted_iota(jnp.int32, (probes, cols), 1)

    def sort_block(block, carry):
        first = block * pair
        values, slopes = [], []
        for row in range(pair + 2):
            cells = rows_all[first + row]
            beside = jnp.where(col_pos == 0, 0.0, pltpu.roll(cells, 1, 1)) + jnp.where(
                col_pos == cols - 1, 0.0, pltpu.roll(cells, cols - 1, 1)
            )
            values.append(line_ref[0:1, :] * cells + line_ref[2:3, :] * beside)
            slopes.append(line_ref[1:2, :] * cells + line_ref[3:4, :] * beside)

        def segment(ref, row):
            at = first * parts + row * parts
            return jnp.concatenate(
                [ref[pl.ds(at + part, 1), :] for part in range(parts)], axis=1
            )

        blocks_of = []
        for row in range(pair):
            pos = first_row + first + row
            edge = (pos == 0) | (pos == trial_rows - 1)
            row_diag = jnp.where(edge, line_ref[6:7, :], line_ref[7:8, :])
            row_slope_diag = jnp.where(edge, line_ref[8:9, :], line_ref[9:10, :])
            scale = jnp.where(pos < trial_rows, line_ref[10:11, :], 0.0)
            row_off, row_slope_off = line_ref[4:5, :], line_ref[5:6, :]
            value_beside = values[row] + values[row + 2]
            slope_beside = slopes[row] + slopes[row + 2]
            three = jnp.concatenate(
                [
                    (row_diag * values[row + 1] + row_off * value_beside) * scale,
                    (row_slope_diag * values[row + 1] + row_slope_off * value_beside) * scale,
                    (row_diag * slopes[row + 1] + row_off * slope_beside) * scale,
                ],
                axis=0,
            )
            member = segment(member_ref, row)
            slot = jnp.bitwise_and(segment(slot_ref, row), G_DEV // HALVES - 1)
            code_row = lax.broadcasted_iota(jnp.int32, (TILE, cols), 0)
            code = jnp.where(
                jnp.bitwise_and(code_row, 1) == 0, lax.div(slot, CODE), lax.rem(slot, CODE)
            ).astype(jnp.float32)
            masked = []
            for index in range(MEMBERS):
                masked.append(jnp.where(member == index, three, 0.0))
                masked.append(code)
            blocks_of.append(jnp.concatenate(masked, axis=0).astype(jnp.bfloat16))
        payload = jnp.concatenate(blocks_of, axis=1)
        place = jnp.concatenate([segment(place_ref, row) for row in range(pair)], axis=1)
        chosen = (
            lax.broadcasted_iota(jnp.int32, (staged, BLOCK * LANES), 0) == place
        ).astype(jnp.bfloat16)
        ordered = lax.dot_general(
            chosen, payload, (((1,), (1,)), ((), ())), preferred_element_type=jnp.float32
        ).astype(jnp.bfloat16)
        for tile in range(staged_tiles):
            goal = pl.multiple_of(table_ref[block, tile] * TILE, TILE)
            bucket[pl.ds(goal, TILE), :] = ordered[tile * TILE : (tile + 1) * TILE, :]
        return carry

    lax.fori_loop(0, blocks, sort_block, 0, unroll=UNROLL)
    end = table_ref[blocks + 6, 2]
    clear = jnp.zeros((TILE, bucket.shape[1]), jnp.bfloat16)
    for tile in range(CHUNK // TILE):
        bucket[pl.ds(pl.multiple_of((end + tile) * TILE, TILE), TILE), :] = clear
    sum_groups(0, blocks, terms, table_ref, bucket, acc, [send_ref])


def keep_kernel(blocks, table_ref, bucket, *refs):
    stores, acc = refs[:-1], refs[-1]
    terms = sum(store.shape[2] for store in stores)
    acc[...] = jnp.zeros_like(acc)
    sum_groups(1, blocks, terms, table_ref, bucket, acc, stores)


def exchange(block, axis, bit):
    count = lax.axis_size(axis)
    return lax.ppermute(block, axis, [(i, i ^ bit) for i in range(count)])


def halve(total, names, name):
    at = names.index(name)
    mine = lax.index_in_dim(total, 0, at, keepdims=False)
    other = lax.index_in_dim(total, 1, at, keepdims=False).astype(jnp.bfloat16)
    return mine + exchange(other, *name).astype(jnp.float32), names[:at] + names[at + 1 :]


def body(probe_signs, trial_rows, trial_cols, ar_rho, res_var, plot_owner, plot_slot):
    probes, rows, cols = probe_signs.shape[0], probe_signs.shape[3], probe_signs.shape[4]
    trials, bands = lax.axis_size("trial"), lax.axis_size("geno")
    devices = trials * bands
    terms = 3 * probes
    stride = terms + TILE
    plots = rows * cols
    segments = plots // LANES
    parts = cols // LANES
    blocks = segments // BLOCK
    groups = devices // OWNERS
    signs = probe_signs.reshape(probes, segments, LANES)
    vmem = pl.BlockSpec(memory_space=pltpu.VMEM)
    smem = pl.BlockSpec(memory_space=pltpu.SMEM)

    edges = jnp.concatenate([signs[:, :parts, :], signs[:, -parts:, :]], axis=1)
    near, far = (
        lax.ppermute(
            edges,
            "geno",
            [pair for i in range(side, bands - 1, 2) for pair in ((i, i + 1), (i + 1, i))],
        )
        for side in range(2)
    )

    assert BLOCK * LANES // TILE + groups <= LANES and blocks < LANES
    assert plots // CHUNK + groups // 2 + TOGETHER <= LANES
    tiles = blocks * (BLOCK * LANES // TILE + groups)
    trash_tile = tiles + CHUNK // TILE
    bucket_shape = ((trash_tile + 1) * TILE, MEMBERS * stride)
    half = groups // 2
    acc_shape = (half, G_DEV // HALVES, MEMBERS * stride)
    out_shape = (OWNERS, half, terms, G_DEV)
    mib = 1024 * 1024
    bucket_bytes, acc_bytes = 2 * math.prod(bucket_shape), 4 * math.prod(acc_shape)
    plan_shape = (blocks + 8, LANES)
    send, bucket, plan = pl.pallas_call(
        functools.partial(sort_kernel, groups, trash_tile),
        out_shape=[
            jax.ShapeDtypeStruct(out_shape, jnp.bfloat16),
            jax.ShapeDtypeStruct(bucket_shape, jnp.bfloat16),
            jax.ShapeDtypeStruct(plan_shape, jnp.int32),
        ],
        in_specs=[smem] * 3 + [pl.BlockSpec(memory_space=pltpu.HBM)] * 4 + [vmem] * 2,
        out_specs=[vmem] * 3,
        scratch_shapes=[
            pltpu.SMEM((1, 2), jnp.float32),
            pltpu.VMEM((probes, segments, LANES), jnp.int32),
            pltpu.VMEM((segments, LANES), jnp.int32),
            pltpu.VMEM((segments, LANES), jnp.int32),
            pltpu.VMEM((rows + 2, probes, cols), jnp.float32),
            pltpu.VMEM((16, cols), jnp.float32),
            pltpu.VMEM((segments, LANES), jnp.int32),
            pltpu.VMEM((segments, LANES), jnp.int32),
            pltpu.SMEM(plan_shape, jnp.int32),
            pltpu.VMEM((segments * groups, LANES), jnp.float32),
            pltpu.VMEM((segments * groups, LANES), jnp.float32),
            pltpu.VMEM(acc_shape, jnp.float32),
            pltpu.SemaphoreType.DMA((4,)),
            pltpu.SemaphoreType.DMA,
        ],
        compiler_params=pltpu.CompilerParams(
            vmem_limit_bytes=bucket_bytes
            + acc_bytes
            + 2 * math.prod(out_shape)
            + 8 * segments * groups * LANES
            + 10 * mib
        ),
        name="sort_plots",
    )(
        trial_rows,
        trial_cols,
        res_var,
        *[
            pltpu.with_memory_space_constraint(operand, pltpu.HBM)
            for operand in (
                ar_rho,
                signs,
                plot_owner.reshape(segments, LANES),
                plot_slot.reshape(segments, LANES),
            )
        ],
        near,
        far,
    )
    received = exchange(send, "geno", 1)
    keep = pl.pallas_call(
        functools.partial(keep_kernel, blocks),
        out_shape=[jax.ShapeDtypeStruct((OWNERS, half, probes, G_DEV), jnp.float32)] * 3,
        in_specs=[smem, vmem],
        out_specs=[vmem] * 3,
        scratch_shapes=[pltpu.VMEM(acc_shape, jnp.float32)],
        compiler_params=pltpu.CompilerParams(
            vmem_limit_bytes=bucket_bytes + acc_bytes + 4 * math.prod(out_shape) + 6 * mib
        ),
        cost_estimate=pl.CostEstimate(
            flops=2 * plots * MEMBERS * stride * G_DEV // HALVES, bytes_accessed=bucket_bytes, transcendentals=0
        ),
        name="sum_kept",
    )(plan, bucket)
    geno_bits, trial_bits = bands.bit_length() - 1, trials.bit_length() - 1
    names = [("geno", 2)]
    names += [("trial", 1 << i) for i in reversed(range(trial_bits))]
    names += [("geno", 1 << i) for i in reversed(range(2, geno_bits))]
    dims = [("geno", 2)] + [("trial", 1 << i) for i in range(trial_bits)]
    dims += [("geno", 1 << i) for i in range(2, geno_bits)]
    shape = [2] * len(dims)
    keep = [term.reshape(shape + [probes, G_DEV]) for term in keep]
    received = received.reshape(shape + [3, probes, G_DEV])
    lead = min(3, len(dims))
    parts_now = [
        (keep[part] + received[..., part, :, :].astype(jnp.float32), names) for part in range(3)
    ]
    for step in range(len(dims)):
        for part in range(3):
            name = dims[(part - step) % lead] if step < lead else dims[step]
            parts_now[part] = halve(*parts_now[part], name)
    return jnp.stack([total for total, _ in parts_now], 0)


def solution(mesh):
    return jax.shard_map(
        body,
        mesh=mesh,
        in_specs=(
            P(None, ("trial", "geno"), None, None, None),
            P("trial"),
            P("trial"),
            P("trial", None),
            P("trial"),
            P(("trial", "geno"), None, None, None, None),
            P(("trial", "geno"), None, None, None),
        ),
        out_specs=P(None, None, ("trial", "geno")),
        check_vma=False,
    )
```

```python
import functools
import math

import jax
import jax.numpy as jnp
from jax import lax
from jax.experimental import pallas as pl
from jax.experimental.pallas import tpu as pltpu
from jax.sharding import PartitionSpec as P

G_DEV = 1024
TILE = 16
CHUNK = 512
BLOCK = 4
LANES = 128
HALVES = 2
OWNERS = 2
MEMBERS = HALVES * OWNERS
UNROLL = 22
TOGETHER = 8
FIRST = 256
REST = 2
CODE = 32


def round_up(value, step):
    return -(-value // step) * step


def bits_to_field(bits, row_in, col_in):
    return jnp.where(row_in & col_in, 2.0 * bits.astype(jnp.float32) - 1.0, 0.0)


def place_of(size_ref, rows):
    band = lax.axis_index("geno")
    trial_rows = size_ref[0]
    return trial_rows, band * rows, lax.axis_index("trial") * lax.axis_size("geno") + band


def prepare(
    loads,
    groups,
    trash_tile,
    size_ref,
    cols_ref,
    var_ref,
    rho_ref,
    signs_ref,
    near_ref,
    far_ref,
    owner_ref,
    slot_ref,
    field_ref,
    line_ref,
    member_ref,
    place_ref,
    table_ref,
    table_smem,
    hot,
    cum,
    arrived,
):
    rows, probes, cols = field_ref.shape[0] - 2, field_ref.shape[1], field_ref.shape[2]
    parts = cols // LANES
    segments = rows * parts
    blocks = segments // BLOCK
    trial_rows, first_row, device = place_of(size_ref, rows)
    trial_cols = cols_ref[0]
    odd = lax.rem(lax.axis_index("geno"), 2) == 1
    loads[3].wait()
    pos = lax.broadcasted_iota(jnp.int32, (1, cols), 1)
    flat = jnp.zeros((1, cols), jnp.float32)
    rho = flat + rho_ref[0, 1]
    inverse = 1.0 / (1.0 - rho * rho)
    inside = 1.0 + rho * rho
    edge = (pos == 0) | (pos == trial_cols - 1)
    line_ref[0:1, :] = jnp.where(edge, inverse, inverse * inside)
    line_ref[1:2, :] = jnp.where(
        edge, 2.0 * rho * inverse * inverse, 4.0 * rho * inverse * inverse
    )
    line_ref[2:3, :] = -inverse * rho
    line_ref[3:4, :] = -inside * inverse * inverse
    rho = flat + rho_ref[0, 0]
    inverse = 1.0 / (1.0 - rho * rho)
    inside = 1.0 + rho * rho
    line_ref[4:5, :] = -inverse * rho
    line_ref[5:6, :] = -inside * inverse * inverse
    line_ref[6:7, :] = inverse
    line_ref[7:8, :] = inverse * inside
    line_ref[8:9, :] = 2.0 * rho * inverse * inverse
    line_ref[9:10, :] = 4.0 * rho * inverse * inverse
    line_ref[10:11, :] = jnp.where(pos < trial_cols, 1.0 / (flat + var_ref[0]), 0.0)
    loads[1].wait()
    loads[2].wait()
    owner = jnp.bitwise_xor(owner_ref[...], device)
    rest = lax.shift_right_logical(owner, 1)
    group_of = lax.shift_right_logical(rest, 1) + jnp.where(
        jnp.bitwise_and(owner, 1) == 1, 0, groups // 2
    )
    slot = slot_ref[...]
    member_ref[...] = jnp.bitwise_and(rest, 1) * HALVES + jnp.where(
        slot >= G_DEV // HALVES, 1, 0
    )
    group_id = lax.broadcasted_iota(jnp.int32, (groups, LANES), 0)
    for seg in range(segments):
        hot[seg * groups : (seg + 1) * groups, :] = (
            group_of[seg : seg + 1, :] == group_id
        ).astype(jnp.float32)
    square = (LANES, LANES)
    upper = lax.broadcasted_iota(jnp.int32, square, 0) <= lax.broadcasted_iota(jnp.int32, square, 1)
    before = lax.broadcasted_iota(jnp.int32, square, 0) < lax.broadcasted_iota(jnp.int32, square, 1)
    cum[...] = jnp.dot(
        hot[...].astype(jnp.bfloat16),
        upper.astype(jnp.bfloat16),
        preferred_element_type=jnp.float32,
    )
    lane = lax.broadcasted_iota(jnp.int32, (groups, LANES), 1)
    counts = jnp.zeros((groups, LANES), jnp.float32)
    for block in range(blocks):
        total = jnp.zeros((groups, 1), jnp.float32)
        for seg in range(block * BLOCK, (block + 1) * BLOCK):
            total = total + cum[seg * groups : (seg + 1) * groups, LANES - 1 : LANES]
        counts = jnp.where(lane == block, total, counts)
    tiles = jnp.floor((counts + (TILE - 1.0)) * (1.0 / TILE))
    above = (
        lax.broadcasted_iota(jnp.int32, (groups, groups), 1)
        < lax.broadcasted_iota(jnp.int32, (groups, groups), 0)
    ).astype(jnp.bfloat16)
    tiles_bf = tiles.astype(jnp.bfloat16)
    earlier = jnp.dot(tiles_bf, before.astype(jnp.bfloat16), preferred_element_type=jnp.float32)
    starts = jnp.dot(above, tiles_bf, preferred_element_type=jnp.float32)
    base = jnp.sum(starts, axis=1, keepdims=True)
    lane_f = lane.astype(jnp.float32)
    for block in range(blocks):
        start = starts[:, block : block + 1]
        number = tiles[:, block : block + 1]
        offset = start * float(TILE) - 1.0
        for seg in range(block * BLOCK, (block + 1) * BLOCK):
            here = slice(seg * groups, (seg + 1) * groups)
            place_ref[seg : seg + 1, :] = jnp.sum(
                hot[here, :] * (cum[here, :] + offset), axis=0, keepdims=True
            ).astype(jnp.int32)
            offset = offset + cum[here, LANES - 1 : LANES]
        held = (lane_f >= start) & (lane_f < start + number)
        goal = base + earlier[:, block : block + 1] + lane_f - start
        chosen = jnp.sum(jnp.where(held, goal + 1.0, 0.0), axis=0, keepdims=True)
        table_ref[block : block + 1, :] = jnp.where(
            chosen > 0.0, chosen - 1.0, float(trash_tile)
        ).astype(jnp.int32)
    total = earlier[:, blocks : blocks + 1]
    step = float(CHUNK // TILE)
    chunks = jnp.floor((total + (step - 1.0)) * (1.0 / step))
    group_row = lax.broadcasted_iota(jnp.int32, (groups, LANES), 0)
    ends = []
    for half in range(2):
        mine = (group_row >= half * (groups // 2)) & (group_row < (half + 1) * (groups // 2))
        own = jnp.where(mine, chunks, 0.0)
        first = jnp.dot(above, own.astype(jnp.bfloat16), preferred_element_type=jnp.float32)
        held = mine & (lane_f >= first) & (lane_f < first + own)
        index = lane_f - first
        fields = (
            base + step * index,
            (total - step * index) * float(TILE),
            (group_row - half * (groups // 2)).astype(jnp.float32)
            + jnp.where(index == 0.0, float(FIRST), 0.0),
        )
        for row, value in enumerate(fields):
            at = blocks + 3 * half + row
            table_ref[at : at + 1, :] = jnp.sum(
                jnp.where(held, value, 0.0), axis=0, keepdims=True
            ).astype(jnp.int32)
        ends.append(jnp.sum(own, axis=0, keepdims=True))
    table_ref[blocks + 7 : blocks + 8, :] = jnp.sum(
        jnp.where(group_row == lane, chunks, 0.0), axis=0, keepdims=True
    ).astype(jnp.int32)
    every = jnp.sum(total + jnp.zeros((groups, LANES), jnp.float32), axis=0, keepdims=True)
    lane_row = lax.broadcasted_iota(jnp.int32, (1, LANES), 1)
    table_ref[blocks + 6 : blocks + 7, :] = jnp.where(
        lane_row == 0, ends[0], jnp.where(lane_row == 1, ends[1], every)
    ).astype(jnp.int32)
    copy = pltpu.make_async_copy(table_ref, table_smem, arrived)
    copy.start()
    loads[0].wait()
    for part in range(parts):
        col_in = (
            lax.broadcasted_iota(jnp.int32, (probes, LANES), 1) + part * LANES < trial_cols
        )
        here = slice(part * LANES, (part + 1) * LANES)
        for row in range(rows):
            field_ref[row + 1, :, here] = bits_to_field(
                signs_ref[:, row * parts + part, :], first_row + row < trial_rows, col_in
            )
        low = jnp.where(odd, near_ref[:, parts + part, :], far_ref[:, parts + part, :])
        field_ref[0, :, here] = bits_to_field(
            low, (first_row > 0) & (first_row <= trial_rows), col_in
        )
        high = jnp.where(odd, far_ref[:, part, :], near_ref[:, part, :])
        field_ref[rows + 1, :, here] = bits_to_field(
            high, first_row + rows < trial_rows, col_in
        )
    copy.wait()


def sum_groups(half, blocks, terms, table_ref, bucket, acc, stores):
    stride = terms + TILE
    lane = lax.broadcasted_iota(jnp.int32, (LANES, LANES), 1)
    row_lane = lax.broadcasted_iota(jnp.int32, (1, CHUNK), 1)
    fold = LANES // stride

    def add_chunk(chunk):
        start = pl.multiple_of(table_ref[blocks + 3 * half, chunk] * TILE, TILE)
        left = table_ref[blocks + 3 * half + 1, chunk]
        code = table_ref[blocks + 3 * half + 2, chunk]
        group = jnp.bitwise_and(code, FIRST - 1)
        part = bucket[pl.ds(start, CHUNK), :]
        codes = jnp.zeros((LANES, LANES), jnp.float32)
        spots = [(run % fold) * stride + terms + 2 * (run // fold) for run in range(CHUNK // LANES)]
        for run, spot in enumerate(spots):
            held = part[run * LANES : (run + 1) * LANES, 0:LANES].astype(jnp.float32)
            codes = jnp.where((lane == spot) | (lane == spot + 1), held, codes)
        codes = codes.T
        slot = jnp.concatenate(
            [codes[spot : spot + 1, :] * float(CODE) + codes[spot + 1 : spot + 2, :] for spot in spots],
            axis=1,
        ).astype(jnp.int32)
        slot = jnp.where(row_lane < left, slot, -1)
        incidence = (
            lax.broadcasted_iota(jnp.int32, (acc.shape[1], CHUNK), 0) == slot
        ).astype(jnp.bfloat16)
        before = jnp.where(code >= FIRST, 0.0, acc[group])
        acc[group] = before + jnp.dot(incidence, part, preferred_element_type=jnp.float32)

    def add_some(together, first, index, carry):
        for each in range(together):
            add_chunk(first + index * together + each)
        return carry

    number = table_ref[blocks + 6, half]
    most = lax.div(number, TOGETHER)
    lax.fori_loop(0, most, functools.partial(add_some, TOGETHER, 0), 0)
    rest = number - most * TOGETHER
    lax.fori_loop(
        0, lax.div(rest + REST - 1, REST), functools.partial(add_some, REST, most * TOGETHER), 0
    )
    width = acc.shape[1]

    def finish(group, carry):
        any_plots = table_ref[blocks + 7, half * acc.shape[0] + group] > 0
        result = jnp.where(any_plots, acc[group], 0.0).astype(stores[0].dtype).T
        for index in range(MEMBERS):
            at = index * stride
            for store in stores:
                store[
                    index // HALVES, group, :, (index % HALVES) * width : (index % HALVES + 1) * width
                ] = result[at : at + store.shape[2], :]
                at += store.shape[2]
        return carry

    lax.fori_loop(0, acc.shape[0], finish, 0, unroll=min(8, acc.shape[0]))


def sort_kernel(
    groups,
    trash_tile,
    size_ref,
    cols_ref,
    var_ref,
    rho_hbm,
    signs_hbm,
    owner_hbm,
    slot_hbm,
    near_ref,
    far_ref,
    send_ref,
    bucket,
    plan_ref,
    rho_ref,
    signs_ref,
    owner_ref,
    slot_ref,
    rows_all,
    line_ref,
    member_ref,
    place_ref,
    table_ref,
    hot,
    cum,
    acc,
    loaded,
    arrived,
):
    loads = [
        pltpu.make_async_copy(source, target, loaded.at[index])
        for index, (source, target) in enumerate(
            (
                (signs_hbm, signs_ref),
                (owner_hbm, owner_ref),
                (slot_hbm, slot_ref),
                (rho_hbm, rho_ref),
            )
        )
    ]
    for load in loads:
        load.start()
    prepare(
        loads,
        groups,
        trash_tile,
        size_ref,
        cols_ref,
        var_ref,
        rho_ref,
        signs_ref,
        near_ref,
        far_ref,
        owner_ref,
    slot_ref,
        rows_all,
        line_ref,
        member_ref,
        place_ref,
        plan_ref,
        table_ref,
        hot,
        cum,
        arrived,
    )
    rows, probes, cols = rows_all.shape[0] - 2, rows_all.shape[1], rows_all.shape[2]
    parts = cols // LANES
    pair = BLOCK // parts
    terms = 3 * probes
    stride = terms + TILE
    blocks = rows // pair
    staged_tiles = BLOCK * LANES // TILE + groups
    staged = staged_tiles * TILE
    trial_rows, first_row, _ = place_of(size_ref, rows)
    col_pos = lax.broadcasted_iota(jnp.int32, (probes, cols), 1)

    def sort_block(block, carry):
        first = block * pair
        values, slopes = [], []
        for row in range(pair + 2):
            cells = rows_all[first + row]
            beside = jnp.where(col_pos == 0, 0.0, pltpu.roll(cells, 1, 1)) + jnp.where(
                col_pos == cols - 1, 0.0, pltpu.roll(cells, cols - 1, 1)
            )
            values.append(line_ref[0:1, :] * cells + line_ref[2:3, :] * beside)
            slopes.append(line_ref[1:2, :] * cells + line_ref[3:4, :] * beside)

        def segment(ref, row):
            at = first * parts + row * parts
            return jnp.concatenate(
                [ref[pl.ds(at + part, 1), :] for part in range(parts)], axis=1
            )

        blocks_of = []
        for row in range(pair):
            pos = first_row + first + row
            edge = (pos == 0) | (pos == trial_rows - 1)
            row_diag = jnp.where(edge, line_ref[6:7, :], line_ref[7:8, :])
            row_slope_diag = jnp.where(edge, line_ref[8:9, :], line_ref[9:10, :])
            scale = jnp.where(pos < trial_rows, line_ref[10:11, :], 0.0)
            row_off, row_slope_off = line_ref[4:5, :], line_ref[5:6, :]
            value_beside = values[row] + values[row + 2]
            slope_beside = slopes[row] + slopes[row + 2]
            three = jnp.concatenate(
                [
                    (row_diag * values[row + 1] + row_off * value_beside) * scale,
                    (row_slope_diag * values[row + 1] + row_slope_off * value_beside) * scale,
                    (row_diag * slopes[row + 1] + row_off * slope_beside) * scale,
                ],
                axis=0,
            )
            member = segment(member_ref, row)
            slot = jnp.bitwise_and(segment(slot_ref, row), G_DEV // HALVES - 1)
            code_row = lax.broadcasted_iota(jnp.int32, (TILE, cols), 0)
            code = jnp.where(
                jnp.bitwise_and(code_row, 1) == 0, lax.div(slot, CODE), lax.rem(slot, CODE)
            ).astype(jnp.float32)
            masked = []
            for index in range(MEMBERS):
                masked.append(jnp.where(member == index, three, 0.0))
                masked.append(code)
            blocks_of.append(jnp.concatenate(masked, axis=0).astype(jnp.bfloat16))
        payload = jnp.concatenate(blocks_of, axis=1)
        place = jnp.concatenate([segment(place_ref, row) for row in range(pair)], axis=1)
        shape = (TILE, BLOCK * LANES)
        within = (
            lax.broadcasted_iota(jnp.int32, shape, 0) == jnp.bitwise_and(place, TILE - 1)
        ).astype(jnp.bfloat16)
        goes_to = jnp.broadcast_to(
            lax.div(place, TILE).astype(jnp.float32), shape
        ).astype(jnp.bfloat16)
        chosen = jnp.concatenate(
            [
                jnp.where(goes_to == jnp.bfloat16(tile), within, jnp.bfloat16(0.0))
                for tile in range(staged_tiles)
            ],
            axis=0,
        )
        ordered = lax.dot_general(
            chosen, payload, (((1,), (1,)), ((), ())), preferred_element_type=jnp.float32
        ).astype(jnp.bfloat16)
        for tile in range(staged_tiles):
            goal = pl.multiple_of(table_ref[block, tile] * TILE, TILE)
            bucket[pl.ds(goal, TILE), :] = ordered[tile * TILE : (tile + 1) * TILE, :]
        return carry

    lax.fori_loop(0, blocks, sort_block, 0, unroll=UNROLL)
    end = table_ref[blocks + 6, 2]
    clear = jnp.zeros((TILE, bucket.shape[1]), jnp.bfloat16)
    for tile in range(CHUNK // TILE):
        bucket[pl.ds(pl.multiple_of((end + tile) * TILE, TILE), TILE), :] = clear
    sum_groups(0, blocks, terms, table_ref, bucket, acc, [send_ref])


def keep_kernel(blocks, table_ref, bucket, *refs):
    stores, acc = refs[:-1], refs[-1]
    terms = sum(store.shape[2] for store in stores)
    sum_groups(1, blocks, terms, table_ref, bucket, acc, stores)


def exchange(block, axis, bit):
    count = lax.axis_size(axis)
    return lax.ppermute(block, axis, [(i, i ^ bit) for i in range(count)])


def halve(total, names, name):
    at = names.index(name)
    mine = lax.index_in_dim(total, 0, at, keepdims=False)
    other = lax.index_in_dim(total, 1, at, keepdims=False).astype(jnp.bfloat16)
    return mine + exchange(other, *name).astype(jnp.float32), names[:at] + names[at + 1 :]


def body(probe_signs, trial_rows, trial_cols, ar_rho, res_var, plot_owner, plot_slot):
    probes, rows, cols = probe_signs.shape[0], probe_signs.shape[3], probe_signs.shape[4]
    trials, bands = lax.axis_size("trial"), lax.axis_size("geno")
    devices = trials * bands
    terms = 3 * probes
    stride = terms + TILE
    plots = rows * cols
    segments = plots // LANES
    parts = cols // LANES
    blocks = segments // BLOCK
    groups = devices // OWNERS
    signs = probe_signs.reshape(probes, segments, LANES)
    vmem = pl.BlockSpec(memory_space=pltpu.VMEM)
    smem = pl.BlockSpec(memory_space=pltpu.SMEM)

    edges = jnp.concatenate([signs[:, :parts, :], signs[:, -parts:, :]], axis=1)
    near, far = (
        lax.ppermute(
            edges,
            "geno",
            [pair for i in range(side, bands - 1, 2) for pair in ((i, i + 1), (i + 1, i))],
        )
        for side in range(2)
    )

    assert groups // 2 <= FIRST and groups <= LANES
    assert BLOCK * LANES // TILE + groups <= LANES and blocks < LANES
    tiles = blocks * (BLOCK * LANES // TILE + groups)
    assert tiles // (CHUNK // TILE) + groups // 2 + TOGETHER <= LANES
    trash_tile = tiles + CHUNK // TILE
    bucket_shape = ((trash_tile + 1) * TILE, MEMBERS * stride)
    half = groups // 2
    acc_shape = (half, G_DEV // HALVES, MEMBERS * stride)
    out_shape = (OWNERS, half, terms, G_DEV)
    mib = 1024 * 1024
    bucket_bytes, acc_bytes = 2 * math.prod(bucket_shape), 4 * math.prod(acc_shape)
    plan_shape = (blocks + 8, LANES)
    send, bucket, plan = pl.pallas_call(
        functools.partial(sort_kernel, groups, trash_tile),
        out_shape=[
            jax.ShapeDtypeStruct(out_shape, jnp.bfloat16),
            jax.ShapeDtypeStruct(bucket_shape, jnp.bfloat16),
            jax.ShapeDtypeStruct(plan_shape, jnp.int32),
        ],
        in_specs=[smem] * 3 + [pl.BlockSpec(memory_space=pltpu.HBM)] * 4 + [vmem] * 2,
        out_specs=[vmem] * 3,
        scratch_shapes=[
            pltpu.SMEM((1, 2), jnp.float32),
            pltpu.VMEM((probes, segments, LANES), jnp.int32),
            pltpu.VMEM((segments, LANES), jnp.int32),
            pltpu.VMEM((segments, LANES), jnp.int32),
            pltpu.VMEM((rows + 2, probes, cols), jnp.float32),
            pltpu.VMEM((16, cols), jnp.float32),
            pltpu.VMEM((segments, LANES), jnp.int32),
            pltpu.VMEM((segments, LANES), jnp.int32),
            pltpu.SMEM(plan_shape, jnp.int32),
            pltpu.VMEM((segments * groups, LANES), jnp.float32),
            pltpu.VMEM((segments * groups, LANES), jnp.float32),
            pltpu.VMEM(acc_shape, jnp.float32),
            pltpu.SemaphoreType.DMA((4,)),
            pltpu.SemaphoreType.DMA,
        ],
        compiler_params=pltpu.CompilerParams(
            vmem_limit_bytes=bucket_bytes
            + acc_bytes
            + 2 * math.prod(out_shape)
            + 8 * segments * groups * LANES
            + 10 * mib
        ),
        name="sort_plots",
    )(
        trial_rows,
        trial_cols,
        res_var,
        *[
            pltpu.with_memory_space_constraint(operand, pltpu.HBM)
            for operand in (
                ar_rho,
                signs,
                plot_owner.reshape(segments, LANES),
                plot_slot.reshape(segments, LANES),
            )
        ],
        near,
        far,
    )
    received = exchange(send, "geno", 1)
    keep = pl.pallas_call(
        functools.partial(keep_kernel, blocks),
        out_shape=[jax.ShapeDtypeStruct((OWNERS, half, probes, G_DEV), jnp.float32)] * 3,
        in_specs=[smem, vmem],
        out_specs=[vmem] * 3,
        scratch_shapes=[pltpu.VMEM(acc_shape, jnp.float32)],
        compiler_params=pltpu.CompilerParams(
            vmem_limit_bytes=bucket_bytes + acc_bytes + 4 * math.prod(out_shape) + 6 * mib
        ),
        cost_estimate=pl.CostEstimate(
            flops=2 * plots * MEMBERS * stride * G_DEV // HALVES, bytes_accessed=bucket_bytes, transcendentals=0
        ),
        name="sum_kept",
    )(plan, bucket)
    geno_bits, trial_bits = bands.bit_length() - 1, trials.bit_length() - 1
    names = [("geno", 2)]
    names += [("trial", 1 << i) for i in reversed(range(trial_bits))]
    names += [("geno", 1 << i) for i in reversed(range(2, geno_bits))]
    dims = [("geno", 2)] + [("trial", 1 << i) for i in range(trial_bits)]
    dims += [("geno", 1 << i) for i in range(2, geno_bits)]
    shape = [2] * len(dims)
    keep = [term.reshape(shape + [probes, G_DEV]) for term in keep]
    received = received.reshape(shape + [3, probes, G_DEV])
    lead = min(3, len(dims))
    parts_now = [
        (keep[part] + received[..., part, :, :].astype(jnp.float32), names) for part in range(3)
    ]
    for step in range(len(dims)):
        for part in range(3):
            name = dims[(part - step) % lead] if step < lead else dims[step]
            parts_now[part] = halve(*parts_now[part], name)
    return jnp.stack([total for total, _ in parts_now], 0)


def solution(mesh):
    return jax.shard_map(
        body,
        mesh=mesh,
        in_specs=(
            P(None, ("trial", "geno"), None, None, None),
            P("trial"),
            P("trial"),
            P("trial", None),
            P("trial"),
            P(("trial", "geno"), None, None, None, None),
            P(("trial", "geno"), None, None, None),
        ),
        out_specs=P(None, None, ("trial", "geno")),
        check_vma=False,
    )
```

```python
import functools
import math

import jax
import jax.numpy as jnp
from jax import lax
from jax.experimental import pallas as pl
from jax.experimental.pallas import tpu as pltpu
from jax.sharding import PartitionSpec as P

G_DEV = 1024
TILE = 16
CHUNK = 512
BLOCK = 4
LANES = 128
HALVES = 2
OWNERS = 2
MEMBERS = HALVES * OWNERS
UNROLL = 22
TOGETHER = 6
FIRST = 256
REST = 3
CODE = 32


def round_up(value, step):
    return -(-value // step) * step


def bits_to_field(bits, row_in, col_in):
    return jnp.where(row_in & col_in, 2.0 * bits.astype(jnp.float32) - 1.0, 0.0)


def place_of(size_ref, rows):
    band = lax.axis_index("geno")
    trial_rows = size_ref[0]
    return trial_rows, band * rows, lax.axis_index("trial") * lax.axis_size("geno") + band


def prepare(
    loads,
    groups,
    trash_tile,
    size_ref,
    cols_ref,
    var_ref,
    rho_ref,
    signs_ref,
    near_ref,
    far_ref,
    owner_ref,
    slot_ref,
    field_ref,
    line_ref,
    member_ref,
    place_ref,
    table_ref,
    table_smem,
    hot,
    cum,
    arrived,
):
    rows, probes, cols = field_ref.shape[0] - 2, field_ref.shape[1], field_ref.shape[2]
    parts = cols // LANES
    segments = rows * parts
    blocks = segments // BLOCK
    trial_rows, first_row, device = place_of(size_ref, rows)
    trial_cols = cols_ref[0]
    odd = lax.rem(lax.axis_index("geno"), 2) == 1
    loads[1].wait()
    loads[2].wait()
    owner = jnp.bitwise_xor(owner_ref[...], device)
    rest = lax.shift_right_logical(owner, 1)
    group_of = lax.shift_right_logical(rest, 1) + jnp.where(
        jnp.bitwise_and(owner, 1) == 1, 0, groups // 2
    )
    slot = slot_ref[...]
    member_ref[...] = jnp.bitwise_and(rest, 1) * HALVES + jnp.where(
        slot >= G_DEV // HALVES, 1, 0
    )
    group_id = lax.broadcasted_iota(jnp.int32, (groups, LANES), 0)
    for seg in range(segments):
        hot[seg * groups : (seg + 1) * groups, :] = (
            group_of[seg : seg + 1, :] == group_id
        ).astype(jnp.float32)
    square = (LANES, LANES)
    upper = lax.broadcasted_iota(jnp.int32, square, 0) <= lax.broadcasted_iota(jnp.int32, square, 1)
    before = lax.broadcasted_iota(jnp.int32, square, 0) < lax.broadcasted_iota(jnp.int32, square, 1)
    cum[...] = jnp.dot(
        hot[...].astype(jnp.bfloat16),
        upper.astype(jnp.bfloat16),
        preferred_element_type=jnp.float32,
    )
    lane = lax.broadcasted_iota(jnp.int32, (groups, LANES), 1)
    counts = jnp.zeros((groups, LANES), jnp.float32)
    for block in range(blocks):
        total = jnp.zeros((groups, 1), jnp.float32)
        for seg in range(block * BLOCK, (block + 1) * BLOCK):
            total = total + cum[seg * groups : (seg + 1) * groups, LANES - 1 : LANES]
        counts = jnp.where(lane == block, total, counts)
    tiles = jnp.floor((counts + (TILE - 1.0)) * (1.0 / TILE))
    above = (
        lax.broadcasted_iota(jnp.int32, (groups, groups), 1)
        < lax.broadcasted_iota(jnp.int32, (groups, groups), 0)
    ).astype(jnp.bfloat16)
    tiles_bf = tiles.astype(jnp.bfloat16)
    earlier = jnp.dot(tiles_bf, before.astype(jnp.bfloat16), preferred_element_type=jnp.float32)
    starts = jnp.dot(above, tiles_bf, preferred_element_type=jnp.float32)
    base = jnp.sum(starts, axis=1, keepdims=True)
    lane_f = lane.astype(jnp.float32)
    for block in range(blocks):
        start = starts[:, block : block + 1]
        number = tiles[:, block : block + 1]
        offset = start * float(TILE) - 1.0
        for seg in range(block * BLOCK, (block + 1) * BLOCK):
            here = slice(seg * groups, (seg + 1) * groups)
            place_ref[seg : seg + 1, :] = jnp.sum(
                hot[here, :] * (cum[here, :] + offset), axis=0, keepdims=True
            ).astype(jnp.int32)
            offset = offset + cum[here, LANES - 1 : LANES]
        held = (lane_f >= start) & (lane_f < start + number)
        goal = base + earlier[:, block : block + 1] + lane_f - start
        chosen = jnp.sum(jnp.where(held, goal + 1.0, 0.0), axis=0, keepdims=True)
        table_ref[block : block + 1, :] = jnp.where(
            chosen > 0.0, chosen - 1.0, float(trash_tile)
        ).astype(jnp.int32)
    total = earlier[:, blocks : blocks + 1]
    step = float(CHUNK // TILE)
    chunks = jnp.floor((total + (step - 1.0)) * (1.0 / step))
    group_row = lax.broadcasted_iota(jnp.int32, (groups, LANES), 0)
    ends = []
    for half in range(2):
        mine = (group_row >= half * (groups // 2)) & (group_row < (half + 1) * (groups // 2))
        own = jnp.where(mine, chunks, 0.0)
        first = jnp.dot(above, own.astype(jnp.bfloat16), preferred_element_type=jnp.float32)
        held = mine & (lane_f >= first) & (lane_f < first + own)
        index = lane_f - first
        fields = (
            base + step * index,
            (total - step * index) * float(TILE),
            (group_row - half * (groups // 2)).astype(jnp.float32)
            + jnp.where(index == 0.0, float(FIRST), 0.0),
        )
        for row, value in enumerate(fields):
            at = blocks + 3 * half + row
            table_ref[at : at + 1, :] = jnp.sum(
                jnp.where(held, value, 0.0), axis=0, keepdims=True
            ).astype(jnp.int32)
        ends.append(jnp.sum(own, axis=0, keepdims=True))
    table_ref[blocks + 7 : blocks + 8, :] = jnp.sum(
        jnp.where(group_row == lane, chunks, 0.0), axis=0, keepdims=True
    ).astype(jnp.int32)
    every = jnp.sum(total + jnp.zeros((groups, LANES), jnp.float32), axis=0, keepdims=True)
    lane_row = lax.broadcasted_iota(jnp.int32, (1, LANES), 1)
    table_ref[blocks + 6 : blocks + 7, :] = jnp.where(
        lane_row == 0, ends[0], jnp.where(lane_row == 1, ends[1], every)
    ).astype(jnp.int32)
    copy = pltpu.make_async_copy(table_ref, table_smem, arrived)
    copy.start()
    loads[3].wait()
    pos = lax.broadcasted_iota(jnp.int32, (1, cols), 1)
    flat = jnp.zeros((1, cols), jnp.float32)
    rho = flat + rho_ref[0, 1]
    inverse = 1.0 / (1.0 - rho * rho)
    inside = 1.0 + rho * rho
    edge = (pos == 0) | (pos == trial_cols - 1)
    line_ref[0:1, :] = jnp.where(edge, inverse, inverse * inside)
    line_ref[1:2, :] = jnp.where(
        edge, 2.0 * rho * inverse * inverse, 4.0 * rho * inverse * inverse
    )
    line_ref[2:3, :] = -inverse * rho
    line_ref[3:4, :] = -inside * inverse * inverse
    rho = flat + rho_ref[0, 0]
    inverse = 1.0 / (1.0 - rho * rho)
    inside = 1.0 + rho * rho
    line_ref[4:5, :] = -inverse * rho
    line_ref[5:6, :] = -inside * inverse * inverse
    line_ref[6:7, :] = inverse
    line_ref[7:8, :] = inverse * inside
    line_ref[8:9, :] = 2.0 * rho * inverse * inverse
    line_ref[9:10, :] = 4.0 * rho * inverse * inverse
    line_ref[10:11, :] = jnp.where(pos < trial_cols, 1.0 / (flat + var_ref[0]), 0.0)
    loads[0].wait()
    for part in range(parts):
        col_in = (
            lax.broadcasted_iota(jnp.int32, (probes, LANES), 1) + part * LANES < trial_cols
        )
        here = slice(part * LANES, (part + 1) * LANES)
        for row in range(rows):
            field_ref[row + 1, :, here] = bits_to_field(
                signs_ref[:, row * parts + part, :], first_row + row < trial_rows, col_in
            )
        low = jnp.where(odd, near_ref[:, parts + part, :], far_ref[:, parts + part, :])
        field_ref[0, :, here] = bits_to_field(
            low, (first_row > 0) & (first_row <= trial_rows), col_in
        )
        high = jnp.where(odd, far_ref[:, part, :], near_ref[:, part, :])
        field_ref[rows + 1, :, here] = bits_to_field(
            high, first_row + rows < trial_rows, col_in
        )
    copy.wait()


def sum_groups(half, blocks, terms, table_ref, bucket, acc, stores):
    stride = terms + TILE
    lane = lax.broadcasted_iota(jnp.int32, (LANES, LANES), 1)
    row_lane = lax.broadcasted_iota(jnp.int32, (1, CHUNK), 1)
    fold = LANES // stride

    def add_chunk(chunk):
        start = pl.multiple_of(table_ref[blocks + 3 * half, chunk] * TILE, TILE)
        left = table_ref[blocks + 3 * half + 1, chunk]
        code = table_ref[blocks + 3 * half + 2, chunk]
        group = jnp.bitwise_and(code, FIRST - 1)
        part = bucket[pl.ds(start, CHUNK), :]
        codes = jnp.zeros((LANES, LANES), jnp.float32)
        spots = [(run % fold) * stride + terms + 2 * (run // fold) for run in range(CHUNK // LANES)]
        for run, spot in enumerate(spots):
            held = part[run * LANES : (run + 1) * LANES, 0:LANES].astype(jnp.float32)
            codes = jnp.where((lane == spot) | (lane == spot + 1), held, codes)
        codes = codes.T
        slot = jnp.concatenate(
            [codes[spot : spot + 1, :] * float(CODE) + codes[spot + 1 : spot + 2, :] for spot in spots],
            axis=1,
        ).astype(jnp.int32)
        slot = jnp.where(row_lane < left, slot, -1)
        incidence = (
            lax.broadcasted_iota(jnp.int32, (acc.shape[1], CHUNK), 0) == slot
        ).astype(jnp.bfloat16)
        before = jnp.where(code >= FIRST, 0.0, acc[group])
        acc[group] = before + jnp.dot(incidence, part, preferred_element_type=jnp.float32)

    def add_some(together, first, index, carry):
        for each in range(together):
            add_chunk(first + index * together + each)
        return carry

    number = table_ref[blocks + 6, half]
    most = lax.div(number, TOGETHER)
    lax.fori_loop(0, most, functools.partial(add_some, TOGETHER, 0), 0)
    rest = number - most * TOGETHER
    lax.fori_loop(
        0, lax.div(rest + REST - 1, REST), functools.partial(add_some, REST, most * TOGETHER), 0
    )
    width = acc.shape[1]

    def finish(group, carry):
        any_plots = table_ref[blocks + 7, half * acc.shape[0] + group] > 0
        result = jnp.where(any_plots, acc[group], 0.0).astype(stores[0].dtype).T
        for index in range(MEMBERS):
            at = index * stride
            for store in stores:
                store[
                    index // HALVES, group, :, (index % HALVES) * width : (index % HALVES + 1) * width
                ] = result[at : at + store.shape[2], :]
                at += store.shape[2]
        return carry

    lax.fori_loop(0, acc.shape[0], finish, 0, unroll=min(8, acc.shape[0]))


def sort_kernel(
    groups,
    trash_tile,
    size_ref,
    cols_ref,
    var_ref,
    rho_hbm,
    signs_hbm,
    owner_hbm,
    slot_hbm,
    near_ref,
    far_ref,
    send_ref,
    bucket,
    plan_ref,
    rho_ref,
    signs_ref,
    owner_ref,
    slot_ref,
    rows_all,
    line_ref,
    member_ref,
    place_ref,
    table_ref,
    hot,
    cum,
    acc,
    loaded,
    arrived,
):
    loads = [
        pltpu.make_async_copy(source, target, loaded.at[index])
        for index, (source, target) in enumerate(
            (
                (signs_hbm, signs_ref),
                (owner_hbm, owner_ref),
                (slot_hbm, slot_ref),
                (rho_hbm, rho_ref),
            )
        )
    ]
    for load in loads:
        load.start()
    prepare(
        loads,
        groups,
        trash_tile,
        size_ref,
        cols_ref,
        var_ref,
        rho_ref,
        signs_ref,
        near_ref,
        far_ref,
        owner_ref,
    slot_ref,
        rows_all,
        line_ref,
        member_ref,
        place_ref,
        plan_ref,
        table_ref,
        hot,
        cum,
        arrived,
    )
    rows, probes, cols = rows_all.shape[0] - 2, rows_all.shape[1], rows_all.shape[2]
    parts = cols // LANES
    pair = BLOCK // parts
    terms = 3 * probes
    stride = terms + TILE
    blocks = rows // pair
    staged_tiles = BLOCK * LANES // TILE + groups
    staged = staged_tiles * TILE
    trial_rows, first_row, _ = place_of(size_ref, rows)
    col_pos = lax.broadcasted_iota(jnp.int32, (probes, cols), 1)

    def sort_block(block, carry):
        first = block * pair
        values, slopes = [], []
        for row in range(pair + 2):
            cells = rows_all[first + row]
            beside = jnp.where(col_pos == 0, 0.0, pltpu.roll(cells, 1, 1)) + jnp.where(
                col_pos == cols - 1, 0.0, pltpu.roll(cells, cols - 1, 1)
            )
            values.append(line_ref[0:1, :] * cells + line_ref[2:3, :] * beside)
            slopes.append(line_ref[1:2, :] * cells + line_ref[3:4, :] * beside)

        def segment(ref, row):
            at = first * parts + row * parts
            return jnp.concatenate(
                [ref[pl.ds(at + part, 1), :] for part in range(parts)], axis=1
            )

        blocks_of = []
        for row in range(pair):
            pos = first_row + first + row
            edge = (pos == 0) | (pos == trial_rows - 1)
            row_diag = jnp.where(edge, line_ref[6:7, :], line_ref[7:8, :])
            row_slope_diag = jnp.where(edge, line_ref[8:9, :], line_ref[9:10, :])
            scale = jnp.where(pos < trial_rows, line_ref[10:11, :], 0.0)
            row_off, row_slope_off = line_ref[4:5, :], line_ref[5:6, :]
            value_beside = values[row] + values[row + 2]
            slope_beside = slopes[row] + slopes[row + 2]
            three = jnp.concatenate(
                [
                    (row_diag * values[row + 1] + row_off * value_beside) * scale,
                    (row_slope_diag * values[row + 1] + row_slope_off * value_beside) * scale,
                    (row_diag * slopes[row + 1] + row_off * slope_beside) * scale,
                ],
                axis=0,
            )
            member = segment(member_ref, row)
            slot = jnp.bitwise_and(segment(slot_ref, row), G_DEV // HALVES - 1)
            code_row = lax.broadcasted_iota(jnp.int32, (TILE, cols), 0)
            code = jnp.where(
                jnp.bitwise_and(code_row, 1) == 0, lax.div(slot, CODE), lax.rem(slot, CODE)
            ).astype(jnp.float32)
            masked = []
            for index in range(MEMBERS):
                masked.append(jnp.where(member == index, three, 0.0))
                masked.append(code)
            blocks_of.append(jnp.concatenate(masked, axis=0).astype(jnp.bfloat16))
        payload = jnp.concatenate(blocks_of, axis=1)
        place = jnp.concatenate([segment(place_ref, row) for row in range(pair)], axis=1)
        shape = (TILE, BLOCK * LANES)
        within = (
            lax.broadcasted_iota(jnp.int32, shape, 0) == jnp.bitwise_and(place, TILE - 1)
        ).astype(jnp.bfloat16)
        goes_to = jnp.broadcast_to(
            lax.div(place, TILE).astype(jnp.float32), shape
        ).astype(jnp.bfloat16)
        chosen = jnp.concatenate(
            [
                jnp.where(goes_to == jnp.bfloat16(tile), within, jnp.bfloat16(0.0))
                for tile in range(staged_tiles)
            ],
            axis=0,
        )
        ordered = lax.dot_general(
            chosen, payload, (((1,), (1,)), ((), ())), preferred_element_type=jnp.float32
        ).astype(jnp.bfloat16)
        for tile in range(staged_tiles):
            goal = pl.multiple_of(table_ref[block, tile] * TILE, TILE)
            bucket[pl.ds(goal, TILE), :] = ordered[tile * TILE : (tile + 1) * TILE, :]
        return carry

    lax.fori_loop(0, blocks, sort_block, 0, unroll=UNROLL)
    end = table_ref[blocks + 6, 2]
    clear = jnp.zeros((TILE, bucket.shape[1]), jnp.bfloat16)
    for tile in range(CHUNK // TILE):
        bucket[pl.ds(pl.multiple_of((end + tile) * TILE, TILE), TILE), :] = clear
    sum_groups(0, blocks, terms, table_ref, bucket, acc, [send_ref])


def keep_kernel(blocks, table_ref, bucket, *refs):
    stores, acc = refs[:-1], refs[-1]
    terms = sum(store.shape[2] for store in stores)
    sum_groups(1, blocks, terms, table_ref, bucket, acc, stores)


def exchange(block, axis, bit):
    count = lax.axis_size(axis)
    return lax.ppermute(block, axis, [(i, i ^ bit) for i in range(count)])


def halve(total, names, name):
    at = names.index(name)
    mine = lax.index_in_dim(total, 0, at, keepdims=False)
    other = lax.index_in_dim(total, 1, at, keepdims=False).astype(jnp.bfloat16)
    return mine + exchange(other, *name).astype(jnp.float32), names[:at] + names[at + 1 :]


def body(probe_signs, trial_rows, trial_cols, ar_rho, res_var, plot_owner, plot_slot):
    probes, rows, cols = probe_signs.shape[0], probe_signs.shape[3], probe_signs.shape[4]
    trials, bands = lax.axis_size("trial"), lax.axis_size("geno")
    devices = trials * bands
    terms = 3 * probes
    stride = terms + TILE
    plots = rows * cols
    segments = plots // LANES
    parts = cols // LANES
    blocks = segments // BLOCK
    groups = devices // OWNERS
    signs = probe_signs.reshape(probes, segments, LANES)
    vmem = pl.BlockSpec(memory_space=pltpu.VMEM)
    smem = pl.BlockSpec(memory_space=pltpu.SMEM)

    edges = jnp.concatenate([signs[:, :parts, :], signs[:, -parts:, :]], axis=1)
    near, far = (
        lax.ppermute(
            edges,
            "geno",
            [pair for i in range(side, bands - 1, 2) for pair in ((i, i + 1), (i + 1, i))],
        )
        for side in range(2)
    )

    assert groups // 2 <= FIRST and groups <= LANES
    assert BLOCK * LANES // TILE + groups <= LANES and blocks < LANES
    tiles = blocks * (BLOCK * LANES // TILE + groups)
    assert tiles // (CHUNK // TILE) + groups // 2 + TOGETHER <= LANES
    trash_tile = tiles + CHUNK // TILE
    bucket_shape = ((trash_tile + 1) * TILE, MEMBERS * stride)
    half = groups // 2
    acc_shape = (half, G_DEV // HALVES, MEMBERS * stride)
    out_shape = (OWNERS, half, terms, G_DEV)
    mib = 1024 * 1024
    bucket_bytes, acc_bytes = 2 * math.prod(bucket_shape), 4 * math.prod(acc_shape)
    plan_shape = (blocks + 8, LANES)
    send, bucket, plan = pl.pallas_call(
        functools.partial(sort_kernel, groups, trash_tile),
        out_shape=[
            jax.ShapeDtypeStruct(out_shape, jnp.bfloat16),
            jax.ShapeDtypeStruct(bucket_shape, jnp.bfloat16),
            jax.ShapeDtypeStruct(plan_shape, jnp.int32),
        ],
        in_specs=[smem] * 3 + [pl.BlockSpec(memory_space=pltpu.HBM)] * 4 + [vmem] * 2,
        out_specs=[vmem] * 3,
        scratch_shapes=[
            pltpu.SMEM((1, 2), jnp.float32),
            pltpu.VMEM((probes, segments, LANES), jnp.int32),
            pltpu.VMEM((segments, LANES), jnp.int32),
            pltpu.VMEM((segments, LANES), jnp.int32),
            pltpu.VMEM((rows + 2, probes, cols), jnp.float32),
            pltpu.VMEM((16, cols), jnp.float32),
            pltpu.VMEM((segments, LANES), jnp.int32),
            pltpu.VMEM((segments, LANES), jnp.int32),
            pltpu.SMEM(plan_shape, jnp.int32),
            pltpu.VMEM((segments * groups, LANES), jnp.float32),
            pltpu.VMEM((segments * groups, LANES), jnp.float32),
            pltpu.VMEM(acc_shape, jnp.float32),
            pltpu.SemaphoreType.DMA((4,)),
            pltpu.SemaphoreType.DMA,
        ],
        compiler_params=pltpu.CompilerParams(
            vmem_limit_bytes=bucket_bytes
            + acc_bytes
            + 2 * math.prod(out_shape)
            + 8 * segments * groups * LANES
            + 10 * mib
        ),
        name="sort_plots",
    )(
        trial_rows,
        trial_cols,
        res_var,
        *[
            pltpu.with_memory_space_constraint(operand, pltpu.HBM)
            for operand in (
                ar_rho,
                signs,
                plot_owner.reshape(segments, LANES),
                plot_slot.reshape(segments, LANES),
            )
        ],
        near,
        far,
    )
    received = exchange(send, "geno", 1)
    keep = pl.pallas_call(
        functools.partial(keep_kernel, blocks),
        out_shape=[jax.ShapeDtypeStruct((OWNERS, half, probes, G_DEV), jnp.float32)] * 3,
        in_specs=[smem, vmem],
        out_specs=[vmem] * 3,
        scratch_shapes=[pltpu.VMEM(acc_shape, jnp.float32)],
        compiler_params=pltpu.CompilerParams(
            vmem_limit_bytes=bucket_bytes + acc_bytes + 4 * math.prod(out_shape) + 6 * mib
        ),
        cost_estimate=pl.CostEstimate(
            flops=2 * plots * MEMBERS * stride * G_DEV // HALVES, bytes_accessed=bucket_bytes, transcendentals=0
        ),
        name="sum_kept",
    )(plan, bucket)
    geno_bits, trial_bits = bands.bit_length() - 1, trials.bit_length() - 1
    names = [("geno", 2)]
    names += [("trial", 1 << i) for i in reversed(range(trial_bits))]
    names += [("geno", 1 << i) for i in reversed(range(2, geno_bits))]
    dims = [("geno", 2)] + [("trial", 1 << i) for i in range(trial_bits)]
    dims += [("geno", 1 << i) for i in range(2, geno_bits)]
    shape = [2] * len(dims)
    keep = [term.reshape(shape + [probes, G_DEV]) for term in keep]
    received = received.reshape(shape + [3, probes, G_DEV])
    lead = min(3, len(dims))
    parts_now = [
        (keep[part] + received[..., part, :, :].astype(jnp.float32), names) for part in range(3)
    ]
    for step in range(len(dims)):
        for part in range(3):
            name = dims[(part - step) % lead] if step < lead else dims[step]
            parts_now[part] = halve(*parts_now[part], name)
    return jnp.stack([total for total, _ in parts_now], 0)


def solution(mesh):
    return jax.shard_map(
        body,
        mesh=mesh,
        in_specs=(
            P(None, ("trial", "geno"), None, None, None),
            P("trial"),
            P("trial"),
            P("trial", None),
            P("trial"),
            P(("trial", "geno"), None, None, None, None),
            P(("trial", "geno"), None, None, None),
        ),
        out_specs=P(None, None, ("trial", "geno")),
        check_vma=False,
    )
```

```python
import functools
import math

import jax
import jax.numpy as jnp
from jax import lax
from jax.experimental import pallas as pl
from jax.experimental.pallas import tpu as pltpu
from jax.sharding import PartitionSpec as P

G_DEV = 1024
TILE = 16
CHUNK = 512
BLOCK = 4
LANES = 128
HALVES = 2
OWNERS = 2
MEMBERS = HALVES * OWNERS
UNROLL = 22
TOGETHER = 6
FIRST = 256
REST = 3
CODE = 32


def round_up(value, step):
    return -(-value // step) * step


def bits_to_field(bits, row_in, col_in):
    return jnp.where(row_in & col_in, 2.0 * bits.astype(jnp.float32) - 1.0, 0.0)


def place_of(size_ref, rows):
    band = lax.axis_index("geno")
    trial_rows = size_ref[0]
    return trial_rows, band * rows, lax.axis_index("trial") * lax.axis_size("geno") + band


def prepare(
    loads,
    groups,
    trash_tile,
    size_ref,
    cols_ref,
    var_ref,
    rho_ref,
    signs_ref,
    near_ref,
    far_ref,
    owner_ref,
    slot_ref,
    field_ref,
    line_ref,
    member_ref,
    place_ref,
    table_ref,
    table_smem,
    hot,
    cum,
    arrived,
):
    rows, probes, cols = field_ref.shape[0] - 2, field_ref.shape[1], field_ref.shape[2]
    parts = cols // LANES
    segments = rows * parts
    blocks = segments // BLOCK
    trial_rows, first_row, device = place_of(size_ref, rows)
    trial_cols = cols_ref[0]
    odd = lax.rem(lax.axis_index("geno"), 2) == 1
    loads[1].wait()
    loads[2].wait()
    owner = jnp.bitwise_xor(owner_ref[...], device)
    rest = lax.shift_right_logical(owner, 1)
    group_of = lax.shift_right_logical(rest, 1) + jnp.where(
        jnp.bitwise_and(owner, 1) == 1, 0, groups // 2
    )
    slot = slot_ref[...]
    member_ref[...] = jnp.bitwise_and(rest, 1) * HALVES + jnp.where(
        slot >= G_DEV // HALVES, 1, 0
    )
    group_id = lax.broadcasted_iota(jnp.int32, (groups, LANES), 0)
    for seg in range(segments):
        hot[seg * groups : (seg + 1) * groups, :] = (
            group_of[seg : seg + 1, :] == group_id
        ).astype(jnp.float32)
    square = (LANES, LANES)
    upper = lax.broadcasted_iota(jnp.int32, square, 0) <= lax.broadcasted_iota(jnp.int32, square, 1)
    before = lax.broadcasted_iota(jnp.int32, square, 0) < lax.broadcasted_iota(jnp.int32, square, 1)
    cum[...] = jnp.dot(
        hot[...].astype(jnp.bfloat16),
        upper.astype(jnp.bfloat16),
        preferred_element_type=jnp.float32,
    )
    lane = lax.broadcasted_iota(jnp.int32, (groups, LANES), 1)
    counts = jnp.zeros((groups, LANES), jnp.float32)
    for block in range(blocks):
        total = jnp.zeros((groups, 1), jnp.float32)
        for seg in range(block * BLOCK, (block + 1) * BLOCK):
            total = total + cum[seg * groups : (seg + 1) * groups, LANES - 1 : LANES]
        counts = jnp.where(lane == block, total, counts)
    tiles = jnp.floor((counts + (TILE - 1.0)) * (1.0 / TILE))
    above = (
        lax.broadcasted_iota(jnp.int32, (groups, groups), 1)
        < lax.broadcasted_iota(jnp.int32, (groups, groups), 0)
    ).astype(jnp.bfloat16)
    tiles_bf = tiles.astype(jnp.bfloat16)
    earlier = jnp.dot(tiles_bf, before.astype(jnp.bfloat16), preferred_element_type=jnp.float32)
    starts = jnp.dot(above, tiles_bf, preferred_element_type=jnp.float32)
    base = jnp.sum(starts, axis=1, keepdims=True)
    lane_f = lane.astype(jnp.float32)
    for block in range(blocks):
        start = starts[:, block : block + 1]
        number = tiles[:, block : block + 1]
        offset = start * float(TILE) - 1.0
        for seg in range(block * BLOCK, (block + 1) * BLOCK):
            here = slice(seg * groups, (seg + 1) * groups)
            place_ref[seg : seg + 1, :] = jnp.sum(
                hot[here, :] * (cum[here, :] + offset), axis=0, keepdims=True
            ).astype(jnp.int32)
            offset = offset + cum[here, LANES - 1 : LANES]
        held = (lane_f >= start) & (lane_f < start + number)
        goal = base + earlier[:, block : block + 1] + lane_f - start
        chosen = jnp.sum(jnp.where(held, goal + 1.0, 0.0), axis=0, keepdims=True)
        table_ref[block : block + 1, :] = jnp.where(
            chosen > 0.0, chosen - 1.0, float(trash_tile)
        ).astype(jnp.int32)
    total = earlier[:, blocks : blocks + 1]
    step = float(CHUNK // TILE)
    chunks = jnp.floor((total + (step - 1.0)) * (1.0 / step))
    group_row = lax.broadcasted_iota(jnp.int32, (groups, LANES), 0)
    ends = []
    for half in range(2):
        mine = (group_row >= half * (groups // 2)) & (group_row < (half + 1) * (groups // 2))
        own = jnp.where(mine, chunks, 0.0)
        first = jnp.dot(above, own.astype(jnp.bfloat16), preferred_element_type=jnp.float32)
        held = mine & (lane_f >= first) & (lane_f < first + own)
        index = lane_f - first
        fields = (
            base + step * index,
            (total - step * index) * float(TILE),
            (group_row - half * (groups // 2)).astype(jnp.float32)
            + jnp.where(index == 0.0, float(FIRST), 0.0),
        )
        for row, value in enumerate(fields):
            at = blocks + 3 * half + row
            table_ref[at : at + 1, :] = jnp.sum(
                jnp.where(held, value, 0.0), axis=0, keepdims=True
            ).astype(jnp.int32)
        ends.append(jnp.sum(own, axis=0, keepdims=True))
    table_ref[blocks + 7 : blocks + 8, :] = jnp.sum(
        jnp.where(group_row == lane, chunks, 0.0), axis=0, keepdims=True
    ).astype(jnp.int32)
    every = jnp.sum(total + jnp.zeros((groups, LANES), jnp.float32), axis=0, keepdims=True)
    lane_row = lax.broadcasted_iota(jnp.int32, (1, LANES), 1)
    table_ref[blocks + 6 : blocks + 7, :] = jnp.where(
        lane_row == 0, ends[0], jnp.where(lane_row == 1, ends[1], every)
    ).astype(jnp.int32)
    copy = pltpu.make_async_copy(table_ref, table_smem, arrived)
    copy.start()
    loads[3].wait()
    pos = lax.broadcasted_iota(jnp.int32, (1, cols), 1)
    flat = jnp.zeros((1, cols), jnp.float32)
    rho = flat + rho_ref[0, 1]
    inverse = 1.0 / (1.0 - rho * rho)
    inside = 1.0 + rho * rho
    edge = (pos == 0) | (pos == trial_cols - 1)
    line_ref[0:1, :] = jnp.where(edge, inverse, inverse * inside)
    line_ref[1:2, :] = jnp.where(
        edge, 2.0 * rho * inverse * inverse, 4.0 * rho * inverse * inverse
    )
    line_ref[2:3, :] = -inverse * rho
    line_ref[3:4, :] = -inside * inverse * inverse
    rho = flat + rho_ref[0, 0]
    inverse = 1.0 / (1.0 - rho * rho)
    inside = 1.0 + rho * rho
    line_ref[4:5, :] = -inverse * rho
    line_ref[5:6, :] = -inside * inverse * inverse
    line_ref[6:7, :] = inverse
    line_ref[7:8, :] = inverse * inside
    line_ref[8:9, :] = 2.0 * rho * inverse * inverse
    line_ref[9:10, :] = 4.0 * rho * inverse * inverse
    line_ref[10:11, :] = jnp.where(pos < trial_cols, 1.0 / (flat + var_ref[0]), 0.0)
    loads[0].wait()
    for part in range(parts):
        col_in = (
            lax.broadcasted_iota(jnp.int32, (probes, LANES), 1) + part * LANES < trial_cols
        )
        here = slice(part * LANES, (part + 1) * LANES)
        for row in range(rows):
            field_ref[row + 1, :, here] = bits_to_field(
                signs_ref[:, row * parts + part, :], first_row + row < trial_rows, col_in
            )
        low = jnp.where(odd, near_ref[:, parts + part, :], far_ref[:, parts + part, :])
        field_ref[0, :, here] = bits_to_field(
            low, (first_row > 0) & (first_row <= trial_rows), col_in
        )
        high = jnp.where(odd, far_ref[:, part, :], near_ref[:, part, :])
        field_ref[rows + 1, :, here] = bits_to_field(
            high, first_row + rows < trial_rows, col_in
        )
    copy.wait()


def sum_groups(half, blocks, terms, table_ref, bucket, acc, stores):
    stride = terms + TILE
    lane = lax.broadcasted_iota(jnp.int32, (LANES, LANES), 1)
    row_lane = lax.broadcasted_iota(jnp.int32, (1, CHUNK), 1)
    fold = LANES // stride

    def add_chunk(chunk):
        start = pl.multiple_of(table_ref[blocks + 3 * half, chunk] * TILE, TILE)
        left = table_ref[blocks + 3 * half + 1, chunk]
        code = table_ref[blocks + 3 * half + 2, chunk]
        group = jnp.bitwise_and(code, FIRST - 1)
        part = bucket[pl.ds(start, CHUNK), :]
        codes = jnp.zeros((LANES, LANES), jnp.float32)
        spots = [(run % fold) * stride + terms + 2 * (run // fold) for run in range(CHUNK // LANES)]
        for run, spot in enumerate(spots):
            held = part[run * LANES : (run + 1) * LANES, 0:LANES].astype(jnp.float32)
            codes = jnp.where((lane == spot) | (lane == spot + 1), held, codes)
        codes = codes.T
        slot = jnp.concatenate(
            [codes[spot : spot + 1, :] * float(CODE) + codes[spot + 1 : spot + 2, :] for spot in spots],
            axis=1,
        ).astype(jnp.int32)
        slot = jnp.where(row_lane < left, slot, -1)
        incidence = (
            lax.broadcasted_iota(jnp.int32, (acc.shape[1], CHUNK), 0) == slot
        ).astype(jnp.bfloat16)
        before = jnp.where(code >= FIRST, 0.0, acc[group])
        acc[group] = before + jnp.dot(incidence, part, preferred_element_type=jnp.float32)

    def add_some(together, first, index, carry):
        for each in range(together):
            add_chunk(first + index * together + each)
        return carry

    number = table_ref[blocks + 6, half]
    most = lax.div(number, TOGETHER)
    lax.fori_loop(0, most, functools.partial(add_some, TOGETHER, 0), 0)
    rest = number - most * TOGETHER
    lax.fori_loop(
        0, lax.div(rest + REST - 1, REST), functools.partial(add_some, REST, most * TOGETHER), 0
    )
    width = acc.shape[1]

    def finish(group, carry):
        any_plots = table_ref[blocks + 7, half * acc.shape[0] + group] > 0
        result = jnp.where(any_plots, acc[group], 0.0).astype(stores[0].dtype).T
        for index in range(MEMBERS):
            at = index * stride
            for store in stores:
                store[
                    index // HALVES, group, :, (index % HALVES) * width : (index % HALVES + 1) * width
                ] = result[at : at + store.shape[2], :]
                at += store.shape[2]
        return carry

    lax.fori_loop(0, acc.shape[0], finish, 0, unroll=min(8, acc.shape[0]))


def sort_kernel(
    groups,
    trash_tile,
    size_ref,
    cols_ref,
    var_ref,
    rho_hbm,
    signs_hbm,
    owner_hbm,
    slot_hbm,
    near_ref,
    far_ref,
    send_ref,
    bucket,
    plan_ref,
    rho_ref,
    signs_ref,
    owner_ref,
    slot_ref,
    rows_all,
    line_ref,
    member_ref,
    place_ref,
    table_ref,
    hot,
    cum,
    acc,
    loaded,
    arrived,
):
    loads = [
        pltpu.make_async_copy(source, target, loaded.at[index])
        for index, (source, target) in enumerate(
            (
                (signs_hbm, signs_ref),
                (owner_hbm, owner_ref),
                (slot_hbm, slot_ref),
                (rho_hbm, rho_ref),
            )
        )
    ]
    for load in loads[1:] + loads[:1]:
        load.start()
    prepare(
        loads,
        groups,
        trash_tile,
        size_ref,
        cols_ref,
        var_ref,
        rho_ref,
        signs_ref,
        near_ref,
        far_ref,
        owner_ref,
    slot_ref,
        rows_all,
        line_ref,
        member_ref,
        place_ref,
        plan_ref,
        table_ref,
        hot,
        cum,
        arrived,
    )
    rows, probes, cols = rows_all.shape[0] - 2, rows_all.shape[1], rows_all.shape[2]
    parts = cols // LANES
    pair = BLOCK // parts
    terms = 3 * probes
    stride = terms + TILE
    blocks = rows // pair
    staged_tiles = BLOCK * LANES // TILE + groups
    staged = staged_tiles * TILE
    trial_rows, first_row, _ = place_of(size_ref, rows)
    col_pos = lax.broadcasted_iota(jnp.int32, (probes, cols), 1)

    def sort_block(block, carry):
        first = block * pair
        values, slopes = [], []
        for row in range(pair + 2):
            cells = rows_all[first + row]
            beside = jnp.where(col_pos == 0, 0.0, pltpu.roll(cells, 1, 1)) + jnp.where(
                col_pos == cols - 1, 0.0, pltpu.roll(cells, cols - 1, 1)
            )
            values.append(line_ref[0:1, :] * cells + line_ref[2:3, :] * beside)
            slopes.append(line_ref[1:2, :] * cells + line_ref[3:4, :] * beside)

        def segment(ref, row):
            at = first * parts + row * parts
            return jnp.concatenate(
                [ref[pl.ds(at + part, 1), :] for part in range(parts)], axis=1
            )

        blocks_of = []
        for row in range(pair):
            pos = first_row + first + row
            edge = (pos == 0) | (pos == trial_rows - 1)
            row_diag = jnp.where(edge, line_ref[6:7, :], line_ref[7:8, :])
            row_slope_diag = jnp.where(edge, line_ref[8:9, :], line_ref[9:10, :])
            scale = jnp.where(pos < trial_rows, line_ref[10:11, :], 0.0)
            row_off, row_slope_off = line_ref[4:5, :], line_ref[5:6, :]
            value_beside = values[row] + values[row + 2]
            slope_beside = slopes[row] + slopes[row + 2]
            three = jnp.concatenate(
                [
                    (row_diag * values[row + 1] + row_off * value_beside) * scale,
                    (row_slope_diag * values[row + 1] + row_slope_off * value_beside) * scale,
                    (row_diag * slopes[row + 1] + row_off * slope_beside) * scale,
                ],
                axis=0,
            )
            member = segment(member_ref, row)
            slot = jnp.bitwise_and(segment(slot_ref, row), G_DEV // HALVES - 1)
            code_row = lax.broadcasted_iota(jnp.int32, (TILE, cols), 0)
            code = jnp.where(
                jnp.bitwise_and(code_row, 1) == 0, lax.div(slot, CODE), lax.rem(slot, CODE)
            ).astype(jnp.float32)
            masked = []
            for index in range(MEMBERS):
                masked.append(jnp.where(member == index, three, 0.0))
                masked.append(code)
            blocks_of.append(jnp.concatenate(masked, axis=0).astype(jnp.bfloat16))
        payload = jnp.concatenate(blocks_of, axis=1)
        place = jnp.concatenate([segment(place_ref, row) for row in range(pair)], axis=1)
        shape = (TILE, BLOCK * LANES)
        within = (
            lax.broadcasted_iota(jnp.int32, shape, 0) == jnp.bitwise_and(place, TILE - 1)
        ).astype(jnp.bfloat16)
        goes_to = jnp.broadcast_to(
            lax.div(place, TILE).astype(jnp.float32), shape
        ).astype(jnp.bfloat16)
        chosen = jnp.concatenate(
            [
                jnp.where(goes_to == jnp.bfloat16(tile), within, jnp.bfloat16(0.0))
                for tile in range(staged_tiles)
            ],
            axis=0,
        )
        ordered = lax.dot_general(
            chosen, payload, (((1,), (1,)), ((), ())), preferred_element_type=jnp.float32
        ).astype(jnp.bfloat16)
        for tile in range(staged_tiles):
            goal = pl.multiple_of(table_ref[block, tile] * TILE, TILE)
            bucket[pl.ds(goal, TILE), :] = ordered[tile * TILE : (tile + 1) * TILE, :]
        return carry

    lax.fori_loop(0, blocks, sort_block, 0, unroll=UNROLL)
    end = table_ref[blocks + 6, 2]
    clear = jnp.zeros((TILE, bucket.shape[1]), jnp.bfloat16)
    for tile in range(CHUNK // TILE):
        bucket[pl.ds(pl.multiple_of((end + tile) * TILE, TILE), TILE), :] = clear
    sum_groups(0, blocks, terms, table_ref, bucket, acc, [send_ref])


def keep_kernel(blocks, table_ref, bucket, *refs):
    stores, acc = refs[:-1], refs[-1]
    terms = sum(store.shape[2] for store in stores)
    sum_groups(1, blocks, terms, table_ref, bucket, acc, stores)


def exchange(block, axis, bit):
    count = lax.axis_size(axis)
    return lax.ppermute(block, axis, [(i, i ^ bit) for i in range(count)])


def halve(total, names, name):
    at = names.index(name)
    mine = lax.index_in_dim(total, 0, at, keepdims=False)
    other = lax.index_in_dim(total, 1, at, keepdims=False).astype(jnp.bfloat16)
    return mine + exchange(other, *name).astype(jnp.float32), names[:at] + names[at + 1 :]


def body(probe_signs, trial_rows, trial_cols, ar_rho, res_var, plot_owner, plot_slot):
    probes, rows, cols = probe_signs.shape[0], probe_signs.shape[3], probe_signs.shape[4]
    trials, bands = lax.axis_size("trial"), lax.axis_size("geno")
    devices = trials * bands
    terms = 3 * probes
    stride = terms + TILE
    plots = rows * cols
    segments = plots // LANES
    parts = cols // LANES
    blocks = segments // BLOCK
    groups = devices // OWNERS
    signs = probe_signs.reshape(probes, segments, LANES)
    vmem = pl.BlockSpec(memory_space=pltpu.VMEM)
    smem = pl.BlockSpec(memory_space=pltpu.SMEM)

    edges = jnp.concatenate([signs[:, :parts, :], signs[:, -parts:, :]], axis=1)
    near, far = (
        lax.ppermute(
            edges,
            "geno",
            [pair for i in range(side, bands - 1, 2) for pair in ((i, i + 1), (i + 1, i))],
        )
        for side in range(2)
    )

    assert groups // 2 <= FIRST and groups <= LANES
    assert BLOCK * LANES // TILE + groups <= LANES and blocks < LANES
    tiles = blocks * (BLOCK * LANES // TILE + groups)
    assert tiles // (CHUNK // TILE) + groups // 2 + TOGETHER <= LANES
    trash_tile = tiles + CHUNK // TILE
    bucket_shape = ((trash_tile + 1) * TILE, MEMBERS * stride)
    half = groups // 2
    acc_shape = (half, G_DEV // HALVES, MEMBERS * stride)
    out_shape = (OWNERS, half, terms, G_DEV)
    mib = 1024 * 1024
    bucket_bytes, acc_bytes = 2 * math.prod(bucket_shape), 4 * math.prod(acc_shape)
    plan_shape = (blocks + 8, LANES)
    send, bucket, plan = pl.pallas_call(
        functools.partial(sort_kernel, groups, trash_tile),
        out_shape=[
            jax.ShapeDtypeStruct(out_shape, jnp.bfloat16),
            jax.ShapeDtypeStruct(bucket_shape, jnp.bfloat16),
            jax.ShapeDtypeStruct(plan_shape, jnp.int32),
        ],
        in_specs=[smem] * 3 + [pl.BlockSpec(memory_space=pltpu.HBM)] * 4 + [vmem] * 2,
        out_specs=[vmem] * 3,
        scratch_shapes=[
            pltpu.SMEM((1, 2), jnp.float32),
            pltpu.VMEM((probes, segments, LANES), jnp.int32),
            pltpu.VMEM((segments, LANES), jnp.int32),
            pltpu.VMEM((segments, LANES), jnp.int32),
            pltpu.VMEM((rows + 2, probes, cols), jnp.float32),
            pltpu.VMEM((16, cols), jnp.float32),
            pltpu.VMEM((segments, LANES), jnp.int32),
            pltpu.VMEM((segments, LANES), jnp.int32),
            pltpu.SMEM(plan_shape, jnp.int32),
            pltpu.VMEM((segments * groups, LANES), jnp.float32),
            pltpu.VMEM((segments * groups, LANES), jnp.float32),
            pltpu.VMEM(acc_shape, jnp.float32),
            pltpu.SemaphoreType.DMA((4,)),
            pltpu.SemaphoreType.DMA,
        ],
        compiler_params=pltpu.CompilerParams(
            vmem_limit_bytes=bucket_bytes
            + acc_bytes
            + 2 * math.prod(out_shape)
            + 8 * segments * groups * LANES
            + 10 * mib
        ),
        name="sort_plots",
    )(
        trial_rows,
        trial_cols,
        res_var,
        *[
            pltpu.with_memory_space_constraint(operand, pltpu.HBM)
            for operand in (
                ar_rho,
                signs,
                plot_owner.reshape(segments, LANES),
                plot_slot.reshape(segments, LANES),
            )
        ],
        near,
        far,
    )
    received = exchange(send, "geno", 1)
    keep = pl.pallas_call(
        functools.partial(keep_kernel, blocks),
        out_shape=[jax.ShapeDtypeStruct((OWNERS, half, probes, G_DEV), jnp.float32)] * 3,
        in_specs=[smem, vmem],
        out_specs=[vmem] * 3,
        scratch_shapes=[pltpu.VMEM(acc_shape, jnp.float32)],
        compiler_params=pltpu.CompilerParams(
            vmem_limit_bytes=bucket_bytes + acc_bytes + 4 * math.prod(out_shape) + 6 * mib
        ),
        cost_estimate=pl.CostEstimate(
            flops=2 * plots * MEMBERS * stride * G_DEV // HALVES, bytes_accessed=bucket_bytes, transcendentals=0
        ),
        name="sum_kept",
    )(plan, bucket)
    geno_bits, trial_bits = bands.bit_length() - 1, trials.bit_length() - 1
    names = [("geno", 2)]
    names += [("trial", 1 << i) for i in reversed(range(trial_bits))]
    names += [("geno", 1 << i) for i in reversed(range(2, geno_bits))]
    dims = [("geno", 2)] + [("trial", 1 << i) for i in range(trial_bits)]
    dims += [("geno", 1 << i) for i in range(2, geno_bits)]
    shape = [2] * len(dims)
    keep = [term.reshape(shape + [probes, G_DEV]) for term in keep]
    received = received.reshape(shape + [3, probes, G_DEV])
    lead = min(3, len(dims))
    parts_now = [
        (keep[part] + received[..., part, :, :].astype(jnp.float32), names) for part in range(3)
    ]
    for step in range(len(dims)):
        for part in range(3):
            name = dims[(part - step) % lead] if step < lead else dims[step]
            parts_now[part] = halve(*parts_now[part], name)
    return jnp.stack([total for total, _ in parts_now], 0)


def solution(mesh):
    return jax.shard_map(
        body,
        mesh=mesh,
        in_specs=(
            P(None, ("trial", "geno"), None, None, None),
            P("trial"),
            P("trial"),
            P("trial", None),
            P("trial"),
            P(("trial", "geno"), None, None, None, None),
            P(("trial", "geno"), None, None, None),
        ),
        out_specs=P(None, None, ("trial", "geno")),
        check_vma=False,
    )
```
